256 devices in a mesh: lon: 32 (over z, x_hi, core), lat: 8 (over y, x_lo).
Axes of the slice: x: 4 (x_hi: 2, x_lo: 2; x = x_hi * 2 + x_lo), y: 4, z: 8, core: 2. Of those that a mesh axis runs over, the one named last changes fastest.
Arguments:
- u_vel: float32 [3, 768, 8192], P(None, 'lat', 'lon'), may hold values from -3 to 3
- v_vel: float32 [3, 768, 8192], P(None, 'lat', 'lon'), may hold values from -3 to 3
- temp: float32 [3, 768, 8192], P(None, 'lat', 'lon'), may hold values from -5 to 5
- salt: float32 [3, 768, 8192], P(None, 'lat', 'lon'), may hold values from -5 to 5
- levels: int32 [768, 8192], P('lat', 'lon'), may hold values from 1 to 3
- land_sea: int32 [768, 8192], P('lat', 'lon'), may hold values 0 or 1
- coriolis: float32 [768, 8192], P('lat', 'lon'), may hold values from -1.5 to 1.5
- inv_dx: float32 [768, 8192], P('lat', 'lon'), may hold values from 0.5 to 2
- inv_dy: float32 [768, 8192], P('lat', 'lon'), may hold values from 0.5 to 2
Outputs:
- u_next: float32 [3, 768, 8192], P(None, 'lat', 'lon')
- v_next: float32 [3, 768, 8192], P(None, 'lat', 'lon')
- temp_next: float32 [3, 768, 8192], P(None, 'lat', 'lon')
- salt_next: float32 [3, 768, 8192], P(None, 'lat', 'lon')
The draws below stay inside these ranges and needn't reach their ends.
All inputs are finite; a program needn't handle non-finite values. No bound on the sum of `land_sea` on one device may be relied on, other than what follows from the above.
Results may differ from the reference program's by a relative error of at most 0.00002.
Values sent between devices are 32-bit elements; how exact they have to be, the bound alone decides.
No kernel may reach another device: no remote copies, remote signals or barrier semaphores. Data moves between devices by JAX's collectives and lax.ppermute only.
A program may use at most 64 MiB of HBM per device.

```python
import math
import jax
import jax.numpy as jnp

K = 3
STEPS = 4
NY = 768
NX = 8192


def touch_ends(values, own_key, low, high):
    place = [jax.random.randint(jax.random.fold_in(own_key, axis), (), 0, length) for axis, length in enumerate(values.shape)]
    main_axis = values.shape.index(max(values.shape))
    neighbour = place[:main_axis] + [(place[main_axis] + 1) % values.shape[main_axis]] + place[main_axis + 1:]
    return values.at[tuple(place)].set(low).at[tuple(neighbour)].set(high)


def block_scale(stream_key, extent, split, least, top_value):
    level, own = 1.0, jax.random.fold_in(stream_key, 6)
    for dim, shards_of in split:
        heights = jnp.exp(jax.random.uniform(jax.random.fold_in(own, dim), (shards_of,), jnp.float32, least / len(split), top_value / len(split)))
        level = level * jnp.repeat(heights, extent[dim] // shards_of).reshape([-1 if axis == dim else 1 for axis in range(len(extent))])
    return level


def noise(rng, extent, spread, bound, cuts=(), kind=jnp.bfloat16):
    result = spread * jax.random.normal(rng, extent, jnp.float32)
    if cuts:
        result = result * block_scale(rng, extent, cuts, -0.22, 0.18)
    return jnp.clip(result, -bound, bound).astype(kind)


def setup_inputs(seed: int = 0) -> dict:
    seeds = jax.random.split(jax.random.key(seed), 10)
    return {
        "u_vel": noise(seeds[0], (K, NY, NX), 0.5, 3.0, ((1, 8), (2, 32)), jnp.float32),
        "v_vel": noise(seeds[1], (K, NY, NX), 0.5, 3.0, ((1, 8), (2, 32)), jnp.float32),
        "temp": noise(seeds[2], (K, NY, NX), 1.0, 5.0, ((1, 8), (2, 32)), jnp.float32),
        "salt": noise(seeds[3], (K, NY, NX), 1.0, 5.0, ((1, 8), (2, 32)), jnp.float32),
        "levels": touch_ends(jax.random.randint(seeds[4], (NY, NX), 1, K + 1), jax.random.fold_in(seeds[4], 1), 1, K).astype(jnp.int32),
        "land_sea": touch_ends((jax.random.randint(seeds[5], (NY, NX), 0, 5) < 4).astype(jnp.int32), jax.random.fold_in(seeds[5], 1), 0, 1),
        "coriolis": jnp.clip(jax.random.uniform(seeds[6], (NY, NX), jnp.float32, -1.5, 1.5) * block_scale(seeds[6], (NY, NX), ((0, 8), (1, 32)), -0.4, 0.0), -1.5, 1.5),
        "inv_dx": jnp.clip(jnp.exp(math.log(2.0) - 1.3862944 * jax.random.uniform(seeds[7], (NY, NX), jnp.float32) ** block_scale(seeds[7], (NY, NX), ((0, 8), (1, 32)), -0.2, 0.2)), 0.5, 2.0),
        "inv_dy": jnp.clip(jnp.exp(math.log(2.0) - 1.3862944 * jax.random.uniform(seeds[8], (NY, NX), jnp.float32) ** block_scale(seeds[8], (NY, NX), ((0, 8), (1, 32)), -0.2, 0.2)), 0.5, 2.0),
    }


def extend(stack, signs):
    wide = jnp.concatenate([stack[..., -1:], stack, stack[..., :1]], axis=-1)
    ghost = jnp.flip(wide[..., -1:, :], axis=-1) * signs[:, None, None, None]
    bottom = jnp.zeros_like(ghost)
    return jnp.concatenate([bottom, wide, ghost], axis=-2)


def centre_value(a):
    return a[..., 1:-1, 1:-1]


def east(a):
    return a[..., 1:-1, 2:]


def west(a):
    return a[..., 1:-1, :-2]


def north_value(a):
    return a[..., 2:, 1:-1]


def south_value(a):
    return a[..., :-2, 1:-1]


def advance(padded_field, wet_pad, coriolis, inv_dx, inv_dy):
    zonal_padded, meridional_padded, tracer_padded, density_padded = padded_field[0], padded_field[1], padded_field[2], padded_field[3]
    wet_centre_mask = centre_value(wet_pad)
    face_e = wet_centre_mask * east(wet_pad)
    face_w = wet_centre_mask * west(wet_pad)
    face_n = wet_centre_mask * north_value(wet_pad)
    face_s = wet_centre_mask * south_value(wet_pad)
    zonal_centre = centre_value(zonal_padded)
    meridional_centre = centre_value(meridional_padded)
    vel_e = 0.5 * (zonal_centre + east(zonal_padded))
    vel_w = 0.5 * (zonal_centre + west(zonal_padded))
    velocity_north = 0.5 * (meridional_centre + north_value(meridional_padded))
    velocity_south = 0.5 * (meridional_centre + south_value(meridional_padded))

    def laplacian_term(x):
        xc = centre_value(x)
        return (inv_dx * inv_dx * (face_e * (east(x) - xc) - face_w * (xc - west(x)))
                + inv_dy * inv_dy * (face_n * (north_value(x) - xc) - face_s * (xc - south_value(x))))

    def diverge(x):
        xc = centre_value(x)
        return (inv_dx * (vel_e * face_e * 0.5 * (xc + east(x)) - vel_w * face_w * 0.5 * (xc + west(x)))
                + inv_dy * (velocity_north * face_n * 0.5 * (xc + north_value(x)) - velocity_south * face_s * 0.5 * (xc + south_value(x))))

    def zonal_gradient(x):
        xc = centre_value(x)
        return inv_dx * 0.5 * (face_e * (east(x) - xc) + face_w * (xc - west(x)))

    def meridional_gradient(x):
        xc = centre_value(x)
        return inv_dy * 0.5 * (face_n * (north_value(x) - xc) + face_s * (xc - south_value(x)))

    depth = ((jnp.arange(tracer_padded.shape[0]).astype(jnp.float32) + 0.5) / tracer_padded.shape[0])[:, None, None]
    density = -0.8 * tracer_padded * (1.0 + 0.1 * tracer_padded + 0.3 * depth) + 0.7 * density_padded * (1.0 - 0.05 * tracer_padded)
    pressure_field = 0.5 * (jnp.cumsum(density, axis=0) - 0.5 * density)
    temp_new = (centre_value(tracer_padded) + 0.1 * (-diverge(tracer_padded) + 0.3 * laplacian_term(tracer_padded))) * wet_centre_mask
    salt_new = (centre_value(density_padded) + 0.1 * (-diverge(density_padded) + 0.3 * laplacian_term(density_padded))) * wet_centre_mask
    u_new = (zonal_centre + 0.1 * (coriolis * meridional_centre - zonal_gradient(pressure_field) - zonal_centre * zonal_gradient(zonal_padded) - meridional_centre * meridional_gradient(zonal_padded)
                          + 0.3 * laplacian_term(zonal_padded))) * wet_centre_mask
    meridional_updated = (meridional_centre + 0.1 * (-coriolis * zonal_centre - meridional_gradient(pressure_field) - zonal_centre * zonal_gradient(meridional_padded) - meridional_centre * meridional_gradient(meridional_padded)
                          + 0.3 * laplacian_term(meridional_padded))) * wet_centre_mask
    return jnp.stack([u_new, meridional_updated, temp_new, salt_new])


def reference(u_vel, v_vel, temp, salt, levels, land_sea, coriolis, inv_dx, inv_dy):
    layer = jnp.arange(u_vel.shape[0]).astype(jnp.int32)[:, None, None]
    wet = jnp.where((land_sea[None] == 1) & (layer < levels[None]), 1.0, 0.0).astype(jnp.float32)
    wet_pad = extend(wet[None], jnp.ones((1,), jnp.float32))[0]
    signs = jnp.array([-1.0, -1.0, 1.0, 1.0], jnp.float32)
    fields = jnp.stack([u_vel, v_vel, temp, salt])
    for step in range(STEPS):
        fields = advance(extend(fields, signs), wet_pad, coriolis, inv_dx, inv_dy)
    return fields[0], fields[1], fields[2], fields[3]
```

```python
import jax
import jax.numpy as jnp
from jax import lax
from jax.experimental import pallas as pl
from jax.experimental.pallas import tpu as pltpu
from jax.sharding import PartitionSpec as P

STEPS = 4
K = 3
HALO = 4
PLANES = 17
LANES = 128
OFFSET = 16
U, V, T, S, PR = range(5)
CXE, CXW, CYN, CYS, HXE, HXW, HYN, HYS, WET, WCEN, WCOR = range(11)
VMEM_LIMIT = 48 * 1024 * 1024


def plane_values(refs, p, rows, lanes):
    if p < 12:
        return refs[p // 3][p % 3, rows, lanes]
    return refs[4 + p - 12][rows, lanes].astype(jnp.float32)


def lane_index(shape):
    return lax.broadcasted_iota(jnp.int32, shape, len(shape) - 1)


def pack_columns(*refs):
    ins, (out_a, out_b) = refs[:9], refs[9:]
    rows = ins[0].shape[1]
    cols = ins[0].shape[2]
    even = lax.rem(lax.axis_index("lon"), 2) == 0
    lane = lane_index((8, LANES))
    for r in range(0, rows, 8):
        west = east = None
        for p in range(PLANES):
            w = plane_values(ins, p, slice(r, r + 8), slice(0, LANES))
            e = plane_values(ins, p, slice(r, r + 8), slice(cols - LANES, cols))
            w = pltpu.roll(w, 4 * p, 1) if p else w
            e = pltpu.roll(e, (4 * p + HALO) % LANES, 1)
            if p == 0:
                west, east = w, e
            else:
                mine = lane >= 4 * p
                west, east = jnp.where(mine, w, west), jnp.where(mine, e, east)
        out_a[r : r + 8, :] = jnp.where(even, east, west)
        out_b[r : r + 8, :] = jnp.where(even, west, east)


def pack_rows(*refs):
    south, north = refs[0:9], refs[9:18]
    col_a, col_b, out_a, out_b = refs[18:]
    rows = col_a.shape[0]
    even = lax.rem(lax.axis_index("lat"), 2) == 0
    for p in range(PLANES):
        s = plane_values(south, p, slice(0, 8), slice(None))[:HALO]
        n = plane_values(north, p, slice(0, 8), slice(None))[HALO:]
        out_a[4 * p : 4 * p + 4, :] = jnp.where(even, n, s)
        out_b[4 * p : 4 * p + 4, :] = jnp.where(even, s, n)
    for ref, lanes in ((col_a, slice(0, LANES)), (col_b, slice(LANES, 2 * LANES))):
        s = ref[0:HALO, :]
        n = ref[rows - HALO : rows, :]
        out_a[4 * PLANES : 4 * PLANES + 4, lanes] = jnp.where(even, n, s)
        out_b[4 * PLANES : 4 * PLANES + 4, lanes] = jnp.where(even, s, n)


def xor_rows(x, bit):
    row = lax.broadcasted_iota(jnp.int32, x.shape, 0)
    return jnp.where((row & bit) != 0, pltpu.roll(x, bit, 0), pltpu.roll(x, 8 - bit, 0))


def xor_lanes(x, bit):
    lane = lane_index(x.shape)
    if bit == LANES // 2:
        return pltpu.roll(x, bit, 1)
    return jnp.where((lane & bit) != 0, pltpu.roll(x, bit, 1), pltpu.roll(x, LANES - bit, 1))


def fold_rows(ref, out):
    lane = lane_index((8, LANES))
    row = lax.broadcasted_iota(jnp.int32, (8, LANES), 0)
    for r in range(0, 4 * PLANES + 4, 8):
        turned, short = [], []
        for t in range(2):
            x = ref[r : r + 8, t * LANES : (t + 1) * LANES]
            x = xor_rows(xor_rows(x, 1), 2)
            x = xor_lanes(xor_lanes(x, 1), 2)
            short.append(x)
            for bit in (4, 8, 16, 32, 64):
                x = xor_lanes(x, bit)
            turned.append(x)
        for t in range(2):
            x = turned[1 - t]
            if r < 24:
                x = -x
            if r + 8 > 4 * PLANES:
                packed = jnp.where(lane < 24, -short[t], short[t])
                x = jnp.where(row < 4, x, packed)
            out[r : r + 8, t * LANES : (t + 1) * LANES] = x


def shift_east(tiles, last):
    rolled = [pltpu.roll(x, LANES - 1, 1) for x in tiles]
    return [jnp.where(last, rolled[(t + 1) % 3], rolled[t]) for t in range(3)]


def shift_west(tiles, first):
    rolled = [pltpu.roll(x, 1, 1) for x in tiles]
    return [jnp.where(first, rolled[(t + 2) % 3], rolled[t]) for t in range(3)]


def density(t, s, k):
    depth = (k + 0.5) / K
    return t * ((-0.8 - 0.24 * depth) - 0.08 * t - 0.035 * s) + 0.7 * s


def advance_block(field, coef, src, r, write):
    lane = lane_index((8, LANES))
    first, last = lane == 0, lane == LANES - 1
    above = [None] * 3
    for k in range(K):
        def load(f, shift):
            return [field[src, f, k, t, pl.ds(r + shift, 8), :] for t in range(3)]

        c = [load(f, 0) for f in range(5)]
        n = [load(f, 1) for f in range(5)]
        s = [load(f, -1) for f in range(5)]
        e = [shift_east(x, last) for x in c]
        w = [shift_west(x, first) for x in c]
        for t in range(3):
            def get(i):
                return coef[i, k, t, pl.ds(r, 8), :]

            cxe, cxw, cyn, cys = get(CXE), get(CXW), get(CYN), get(CYS)
            hxe, hxw, hyn, hys = get(HXE), get(HXW), get(HYN), get(HYS)
            u, v = c[U][t], c[V][t]
            u2, v2 = u + u, v + v
            ae, aw = cxe - hxe * u2, cxw + hxw * u2
            an, as_ = cyn - hyn * v2, cys + hys * v2
            ac = get(WET) - ((ae + aw) + (an + as_))
            wcor = get(WCOR)
            p = c[PR][t]
            px = hxe * (e[PR][t] - p) + hxw * (p - w[PR][t])
            py = hyn * (n[PR][t] - p) + hys * (p - s[PR][t])

            def combine(f, ac, ae, aw, an, as_):
                return (ac * c[f][t] + (ae * e[f][t] + aw * w[f][t])) + (an * n[f][t] + as_ * s[f][t])

            write(U, k, t, combine(U, ac, ae, aw, an, as_) + (wcor * v - px))
            write(V, k, t, combine(V, ac, ae, aw, an, as_) - (wcor * u + py))
            ae = cxe - hxe * (u + e[U][t])
            aw = cxw + hxw * (u + w[U][t])
            an = cyn - hyn * (v + n[V][t])
            as_ = cys + hys * (v + s[V][t])
            ac = get(WCEN) + ((ae + aw) + (an + as_))
            t_new = combine(T, ac, ae, aw, an, as_)
            s_new = combine(S, ac, ae, aw, an, as_)
            write(T, k, t, t_new)
            write(S, k, t, s_new)
            rho = density(t_new, s_new, k)
            half = 0.5 * rho
            write(PR, k, t, half if k == 0 else above[t] + half)
            above[t] = rho if k == 0 else above[t] + rho


def run_steps(*refs):
    ins, (col_a, col_b, row_a, row_b), outs = refs[:9], refs[9:13], refs[13:17]
    field, coef, wet, geo, cols, north = refs[17:]
    rows = ins[0].shape[1]
    top = OFFSET + rows
    lon_even = lax.rem(lax.axis_index("lon"), 2) == 0
    lat = lax.axis_index("lat")
    lat_even = lax.rem(lat, 2) == 0
    lane = lane_index((8, LANES))
    first, last = lane == 0, lane == LANES - 1

    fold = lat == lax.axis_size("lat") - 1

    @pl.when(fold)
    def _():
        fold_rows(row_b, north)

    @pl.when(jnp.logical_not(fold))
    def _():
        north[...] = jnp.where(lat_even, row_a[...], row_b[...])

    def south_rows(p, lanes):
        rows_p = slice(4 * p, 4 * p + 4)
        return jnp.where(lat_even, row_b[rows_p, lanes], row_a[rows_p, lanes])

    def place(dst, a, b):
        for half, even_ref in ((0, b), (1, a)):
            odd_ref = a if half == 0 else b
            cols[half, dst, :] = jnp.where(lon_even, even_ref, odd_ref)

    place(slice(OFFSET, top), col_a[...], col_b[...])
    rows_c = slice(4 * PLANES, 4 * PLANES + 4)
    place(
        slice(OFFSET - HALO, OFFSET),
        south_rows(PLANES, slice(0, LANES)),
        south_rows(PLANES, slice(LANES, 2 * LANES)),
    )
    place(slice(top, top + HALO), north[rows_c, 0:LANES], north[rows_c, LANES : 2 * LANES])

    def target(p):
        if p < 12:
            return lambda t, dst: (field, (0, p // 3, p % 3, t, dst, slice(None)))
        return lambda t, dst: (geo, (p - 12, t, dst, slice(None)))

    for p in range(PLANES):
        at = target(p)
        for t in range(2):
            lanes = slice(t * LANES, (t + 1) * LANES)
            ref, idx = at(t, slice(OFFSET, top))
            ref[idx] = plane_values(ins, p, slice(None), lanes)
            ref, idx = at(t, slice(OFFSET - HALO, OFFSET))
            ref[idx] = south_rows(p, lanes)
            ref, idx = at(t, slice(top, top + HALO))
            ref[idx] = north[4 * p : 4 * p + 4, lanes]

    @pl.loop(0, (rows + 16) // 8)
    def _(b):
        r = pl.multiple_of(OFFSET - 8 + 8 * b, 8)
        west, east = cols[0, pl.ds(r, 8), :], cols[1, pl.ds(r, 8), :]
        for p in range(PLANES):
            e = pltpu.roll(east, LANES - 4 * p, 1) if p else east
            w = pltpu.roll(west, LANES - 4 * p - HALO, 1)
            ref, idx = target(p)(2, pl.ds(r, 8))
            ref[idx] = jnp.where(lane < LANES // 2, e, w)
        for t in range(3):
            wet_levels = jnp.where(geo[1, t, pl.ds(r, 8), :] == 1.0, geo[0, t, pl.ds(r, 8), :], 0.0)
            above = None
            for k in range(K):
                wet[k, t, pl.ds(r, 8), :] = jnp.where(wet_levels > k, 1.0, 0.0)
                rho = density(field[0, T, k, t, pl.ds(r, 8), :], field[0, S, k, t, pl.ds(r, 8), :], k)
                half = 0.5 * rho
                field[0, PR, k, t, pl.ds(r, 8), :] = half if k == 0 else above + half
                above = rho if k == 0 else above + rho

    @pl.loop(0, (rows + 16) // 8)
    def _(b):
        r = pl.multiple_of(OFFSET - 8 + 8 * b, 8)
        for k in range(K):
            c = [wet[k, t, pl.ds(r, 8), :] for t in range(3)]
            e, w = shift_east(c, last), shift_west(c, first)
            for t in range(3):
                n = wet[k, t, pl.ds(r + 1, 8), :]
                s = wet[k, t, pl.ds(r - 1, 8), :]
                idx, idy = geo[3, t, pl.ds(r, 8), :], geo[4, t, pl.ds(r, 8), :]
                hx, hy = 0.025 * idx, 0.025 * idy
                fe, fw, fn, fs = c[t] * e[t], c[t] * w[t], c[t] * n, c[t] * s
                hxe, hxw, hyn, hys = fe * hx, fw * hx, fn * hy, fs * hy
                cx, cy = 1.2 * idx, 1.2 * idy
                cxe, cxw, cyn, cys = hxe * cx, hxw * cx, hyn * cy, hys * cy
                total = (cxe + cxw) + (cyn + cys)
                for i, value in (
                    (CXE, cxe), (CXW, cxw), (CYN, cyn), (CYS, cys),
                    (HXE, hxe), (HXW, hxw), (HYN, hyn), (HYS, hys),
                    (WET, c[t]), (WCEN, c[t] - 2.0 * total),
                    (WCOR, 0.1 * c[t] * geo[2, t, pl.ds(r, 8), :]),
                ):
                    coef[i, k, t, pl.ds(r, 8), :] = value

    for step in range(STEPS - 1):
        @pl.loop(0, (rows + 16) // 8)
        def _(b):
            r = pl.multiple_of(OFFSET - 8 + 8 * b, 8)

            def write(f, k, t, value):
                field[(step + 1) % 2, f, k, t, pl.ds(r, 8), :] = value

            advance_block(field, coef, step % 2, r, write)

    @pl.loop(0, rows // 8)
    def _(b):
        r = pl.multiple_of(8 * b, 8)

        def write(f, k, t, value):
            if f < PR and t < 2:
                outs[f][k, pl.ds(r, 8), t * LANES : (t + 1) * LANES] = value

        advance_block(field, coef, (STEPS - 1) % 2, pl.multiple_of(OFFSET + r, 8), write)


def lon_pairs(nlon, nlat, partner):
    return [(i * nlat + j, partner(i) * nlat + j) for i in range(nlon) for j in range(nlat)]


def lat_pairs(nlon, nlat, odd):
    pairs = []
    for i in range(nlon):
        for j in range(nlat):
            up = (j % 2 == 0) != odd
            to, at = (j + 1 if up else j - 1), i
            if to < 0:
                continue
            if to == nlat:
                to, at = nlat - 1, nlon - 1 - i
            pairs.append((i * nlat + j, at * nlat + to))
    return pairs


def body(u_vel, v_vel, temp, salt, levels, land_sea, coriolis, inv_dx, inv_dy):
    args = (u_vel, v_vel, temp, salt, levels, land_sea, coriolis, inv_dx, inv_dy)
    rows, cols = levels.shape
    nlon, nlat = lax.axis_size("lon"), lax.axis_size("lat")
    axes = ("lon", "lat")
    params = pltpu.CompilerParams(vmem_limit_bytes=VMEM_LIMIT)
    f32 = jnp.float32
    column = jax.ShapeDtypeStruct((rows, LANES), f32)
    col_a, col_b = pl.pallas_call(
        pack_columns, out_shape=(column, column), compiler_params=params, name="pack_columns"
    )(*args)
    col_a = lax.ppermute(col_a, axes, lon_pairs(nlon, nlat, lambda i: i ^ 1))
    col_b = lax.ppermute(
        col_b, axes, lon_pairs(nlon, nlat, lambda i: (i + 1 if i % 2 else i - 1) % nlon)
    )

    def edge(block):
        def spec(a):
            if a.ndim == 3:
                return pl.BlockSpec((K, 8, cols), lambda i: (0, block, 0))
            return pl.BlockSpec((8, cols), lambda i: (block, 0))
        return [spec(a) for a in args]

    whole = pl.BlockSpec((rows, LANES), lambda i: (0, 0))
    row = jax.ShapeDtypeStruct((4 * PLANES + 4, cols), f32)
    row_spec = pl.BlockSpec(row.shape, lambda i: (0, 0))
    row_a, row_b = pl.pallas_call(
        pack_rows,
        grid=(1,),
        in_specs=edge(0) + edge(rows // 8 - 1) + [whole, whole],
        out_specs=(row_spec, row_spec),
        out_shape=(row, row),
        compiler_params=params,
        name="pack_rows",
    )(*args, *args, col_a, col_b)
    row_b = lax.ppermute(row_b, axes, lat_pairs(nlon, nlat, True))
    row_a = lax.ppermute(row_a, axes, lat_pairs(nlon, nlat, False))
    tall = rows + 32
    out = jax.ShapeDtypeStruct(u_vel.shape, f32)
    return pl.pallas_call(
        run_steps,
        out_shape=(out,) * 4,
        scratch_shapes=[
            pltpu.VMEM((2, 5, K, 3, tall, LANES), f32),
            pltpu.VMEM((11, K, 3, tall, LANES), f32),
            pltpu.VMEM((K, 3, tall, LANES), f32),
            pltpu.VMEM((5, 3, tall, LANES), f32),
            pltpu.VMEM((2, tall, LANES), f32),
            pltpu.VMEM(row.shape, f32),
        ],
        compiler_params=params,
        name="run_steps",
    )(*args, col_a, col_b, row_a, row_b)


def solution(mesh):
    block, plane = P(None, "lat", "lon"), P("lat", "lon")
    return jax.shard_map(
        body,
        mesh=mesh,
        in_specs=(block,) * 4 + (plane,) * 5,
        out_specs=(block,) * 4,
        check_vma=False,
    )
```

```python
import jax
import jax.numpy as jnp
from jax import lax
from jax.experimental import pallas as pl
from jax.experimental.pallas import tpu as pltpu
from jax.sharding import PartitionSpec as P

STEPS = 4
K = 3
HALO = 4
PLANES = 17
LANES = 128
OFFSET = 16
U, V, T, S, PR = range(5)
CXE, CXW, CYN, CYS, HXE, HXW, HYN, HYS, WET, WCEN, WCOR = range(11)
VMEM_LIMIT = 48 * 1024 * 1024


def plane_values(refs, p, rows, lanes):
    if p < 12:
        return refs[p // 3][p % 3, rows, lanes]
    return refs[4 + p - 12][rows, lanes].astype(jnp.float32)


def lane_index(shape):
    return lax.broadcasted_iota(jnp.int32, shape, len(shape) - 1)


def pack_edges(*refs):
    args, (col_a, col_b, row_a, row_b), ins, sems = refs[:9], refs[9:13], refs[13:22], refs[22]
    copies = [pltpu.make_async_copy(a, i, sems.at[n]) for n, (a, i) in enumerate(zip(args, ins))]
    for copy in copies:
        copy.start()
    for copy in copies:
        copy.wait()
    rows, cols = ins[4].shape
    even = lax.rem(lax.axis_index("lon"), 2) == 0
    lane = lane_index((8, LANES))
    for r in range(0, rows, 8):
        west = east = None
        for p in range(PLANES):
            w = plane_values(ins, p, slice(r, r + 8), slice(0, LANES))
            e = plane_values(ins, p, slice(r, r + 8), slice(cols - LANES, cols))
            w = pltpu.roll(w, 4 * p, 1) if p else w
            e = pltpu.roll(e, (4 * p + HALO) % LANES, 1)
            if p == 0:
                west, east = w, e
            else:
                mine = lane >= 4 * p
                west, east = jnp.where(mine, w, west), jnp.where(mine, e, east)
        col_a[r : r + 8, :] = jnp.where(even, east, west)
        col_b[r : r + 8, :] = jnp.where(even, west, east)
    even = lax.rem(lax.axis_index("lat"), 2) == 0
    for p in range(PLANES):
        s = plane_values(ins, p, slice(0, 8), slice(None))[:HALO]
        n = plane_values(ins, p, slice(rows - 8, rows), slice(None))[HALO:]
        row_a[4 * p : 4 * p + 4, :] = jnp.where(even, n, s)
        row_b[4 * p : 4 * p + 4, :] = jnp.where(even, s, n)


def add_corners(col_a, col_b, in_a, in_b, out_a, out_b):
    rows = col_a.shape[0]
    even = lax.rem(lax.axis_index("lat"), 2) == 0
    out_a[...] = in_a[...]
    out_b[...] = in_b[...]
    for ref, lanes in ((col_a, slice(0, LANES)), (col_b, slice(LANES, 2 * LANES))):
        s = ref[0:HALO, :]
        n = ref[rows - HALO : rows, :]
        out_a[4 * PLANES : 4 * PLANES + 4, lanes] = jnp.where(even, n, s)
        out_b[4 * PLANES : 4 * PLANES + 4, lanes] = jnp.where(even, s, n)


def xor_rows(x, bit):
    row = lax.broadcasted_iota(jnp.int32, x.shape, 0)
    return jnp.where((row & bit) != 0, pltpu.roll(x, bit, 0), pltpu.roll(x, 8 - bit, 0))


def xor_lanes(x, bit):
    lane = lane_index(x.shape)
    if bit == LANES // 2:
        return pltpu.roll(x, bit, 1)
    return jnp.where((lane & bit) != 0, pltpu.roll(x, bit, 1), pltpu.roll(x, LANES - bit, 1))


def fold_rows(ref, out):
    lane = lane_index((8, LANES))
    row = lax.broadcasted_iota(jnp.int32, (8, LANES), 0)
    for r in range(0, 4 * PLANES + 4, 8):
        turned, short = [], []
        for t in range(2):
            x = ref[r : r + 8, t * LANES : (t + 1) * LANES]
            x = xor_rows(xor_rows(x, 1), 2)
            x = xor_lanes(xor_lanes(x, 1), 2)
            short.append(x)
            for bit in (4, 8, 16, 32, 64):
                x = xor_lanes(x, bit)
            turned.append(x)
        for t in range(2):
            x = turned[1 - t]
            if r < 24:
                x = -x
            if r + 8 > 4 * PLANES:
                packed = jnp.where(lane < 24, -short[t], short[t])
                x = jnp.where(row < 4, x, packed)
            out[r : r + 8, t * LANES : (t + 1) * LANES] = x


def shift_east(tiles, last):
    rolled = [pltpu.roll(x, LANES - 1, 1) for x in tiles]
    return [jnp.where(last, rolled[(t + 1) % 3], rolled[t]) for t in range(3)]


def shift_west(tiles, first):
    rolled = [pltpu.roll(x, 1, 1) for x in tiles]
    return [jnp.where(first, rolled[(t + 2) % 3], rolled[t]) for t in range(3)]


def density(t, s, k):
    depth = (k + 0.5) / K
    return t * ((-0.8 - 0.24 * depth) - 0.08 * t - 0.035 * s) + 0.7 * s


def advance_block(field, coef, src, r, write):
    lane = lane_index((8, LANES))
    first, last = lane == 0, lane == LANES - 1
    above = [None] * 3
    for k in range(K):
        for t in range(3):
            def get(i):
                return coef[i, k, t, pl.ds(r, 8), :]

            def fld(f, shift=0, tt=t):
                return field[src, f, k, tt, pl.ds(r + shift, 8), :]

            def around(f):
                c = fld(f)
                e = pltpu.roll(jnp.where(first, fld(f, 0, (t + 1) % 3), c), LANES - 1, 1)
                w = pltpu.roll(jnp.where(last, fld(f, 0, (t + 2) % 3), c), 1, 1)
                return c, e, w, fld(f, 1), fld(f, -1)

            cxe, cxw, cyn, cys = get(CXE), get(CXW), get(CYN), get(CYS)
            hxe, hxw, hyn, hys = get(HXE), get(HXW), get(HYN), get(HYS)
            U5, V5 = around(U), around(V)
            u, v = U5[0], V5[0]
            u2, v2 = u + u, v + v
            ae, aw = cxe - hxe * u2, cxw + hxw * u2
            an, as_ = cyn - hyn * v2, cys + hys * v2
            ac = get(WET) - ((ae + aw) + (an + as_))
            wcor = get(WCOR)
            p, pe, pw, pn, ps = around(PR)
            px = hxe * (pe - p) + hxw * (p - pw)
            py = hyn * (pn - p) + hys * (p - ps)

            def combine(X5, ac, ae, aw, an, as_):
                c, e, w, n, s = X5
                return (ac * c + (ae * e + aw * w)) + (an * n + as_ * s)

            write(U, k, t, combine(U5, ac, ae, aw, an, as_) + (wcor * v - px))
            write(V, k, t, combine(V5, ac, ae, aw, an, as_) - (wcor * u + py))
            ae = cxe - hxe * (u + U5[1])
            aw = cxw + hxw * (u + U5[2])
            an = cyn - hyn * (v + V5[3])
            as_ = cys + hys * (v + V5[4])
            ac = get(WCEN) + ((ae + aw) + (an + as_))
            t_new = combine(around(T), ac, ae, aw, an, as_)
            s_new = combine(around(S), ac, ae, aw, an, as_)
            write(T, k, t, t_new)
            write(S, k, t, s_new)
            rho = density(t_new, s_new, k)
            half = 0.5 * rho
            write(PR, k, t, half if k == 0 else above[t] + half)
            above[t] = rho if k == 0 else above[t] + rho


def run_steps(*refs):
    ins, (col_a, col_b, row_a, row_b), outs = refs[:9], refs[9:13], refs[13:17]
    field, coef, wet, geo, cols, north = refs[17:]
    rows = ins[0].shape[1]
    top = OFFSET + rows
    lon_even = lax.rem(lax.axis_index("lon"), 2) == 0
    lat = lax.axis_index("lat")
    lat_even = lax.rem(lat, 2) == 0
    lane = lane_index((8, LANES))
    first, last = lane == 0, lane == LANES - 1

    fold = lat == lax.axis_size("lat") - 1

    @pl.when(fold)
    def _():
        fold_rows(row_b, north)

    @pl.when(jnp.logical_not(fold))
    def _():
        north[...] = jnp.where(lat_even, row_a[...], row_b[...])

    def south_rows(p, lanes):
        rows_p = slice(4 * p, 4 * p + 4)
        return jnp.where(lat_even, row_b[rows_p, lanes], row_a[rows_p, lanes])

    def place(dst, a, b):
        for half, even_ref in ((0, b), (1, a)):
            odd_ref = a if half == 0 else b
            cols[half, dst, :] = jnp.where(lon_even, even_ref, odd_ref)

    place(slice(OFFSET, top), col_a[...], col_b[...])
    rows_c = slice(4 * PLANES, 4 * PLANES + 4)
    place(
        slice(OFFSET - HALO, OFFSET),
        south_rows(PLANES, slice(0, LANES)),
        south_rows(PLANES, slice(LANES, 2 * LANES)),
    )
    place(slice(top, top + HALO), north[rows_c, 0:LANES], north[rows_c, LANES : 2 * LANES])

    def target(p):
        if p < 12:
            return lambda t, dst: (field, (0, p // 3, p % 3, t, dst, slice(None)))
        return lambda t, dst: (geo, (p - 12, t, dst, slice(None)))

    for p in range(PLANES):
        at = target(p)
        for t in range(2):
            lanes = slice(t * LANES, (t + 1) * LANES)
            ref, idx = at(t, slice(OFFSET, top))
            ref[idx] = plane_values(ins, p, slice(None), lanes)
            ref, idx = at(t, slice(OFFSET - HALO, OFFSET))
            ref[idx] = south_rows(p, lanes)
            ref, idx = at(t, slice(top, top + HALO))
            ref[idx] = north[4 * p : 4 * p + 4, lanes]

    @pl.loop(0, (rows + 16) // 8)
    def _(b):
        r = pl.multiple_of(OFFSET - 8 + 8 * b, 8)
        west, east = cols[0, pl.ds(r, 8), :], cols[1, pl.ds(r, 8), :]
        for p in range(PLANES):
            e = pltpu.roll(east, LANES - 4 * p, 1) if p else east
            w = pltpu.roll(west, LANES - 4 * p - HALO, 1)
            ref, idx = target(p)(2, pl.ds(r, 8))
            ref[idx] = jnp.where(lane < LANES // 2, e, w)
        for t in range(3):
            wet_levels = jnp.where(geo[1, t, pl.ds(r, 8), :] == 1.0, geo[0, t, pl.ds(r, 8), :], 0.0)
            above = None
            for k in range(K):
                wet[k, t, pl.ds(r, 8), :] = jnp.where(wet_levels > k, 1.0, 0.0)
                rho = density(field[0, T, k, t, pl.ds(r, 8), :], field[0, S, k, t, pl.ds(r, 8), :], k)
                half = 0.5 * rho
                field[0, PR, k, t, pl.ds(r, 8), :] = half if k == 0 else above + half
                above = rho if k == 0 else above + rho

    @pl.loop(0, (rows + 16) // 8)
    def _(b):
        r = pl.multiple_of(OFFSET - 8 + 8 * b, 8)
        for k in range(K):
            c = [wet[k, t, pl.ds(r, 8), :] for t in range(3)]
            e, w = shift_east(c, last), shift_west(c, first)
            for t in range(3):
                n = wet[k, t, pl.ds(r + 1, 8), :]
                s = wet[k, t, pl.ds(r - 1, 8), :]
                idx, idy = geo[3, t, pl.ds(r, 8), :], geo[4, t, pl.ds(r, 8), :]
                hx, hy = 0.025 * idx, 0.025 * idy
                fe, fw, fn, fs = c[t] * e[t], c[t] * w[t], c[t] * n, c[t] * s
                hxe, hxw, hyn, hys = fe * hx, fw * hx, fn * hy, fs * hy
                cx, cy = 1.2 * idx, 1.2 * idy
                cxe, cxw, cyn, cys = hxe * cx, hxw * cx, hyn * cy, hys * cy
                total = (cxe + cxw) + (cyn + cys)
                for i, value in (
                    (CXE, cxe), (CXW, cxw), (CYN, cyn), (CYS, cys),
                    (HXE, hxe), (HXW, hxw), (HYN, hyn), (HYS, hys),
                    (WET, c[t]), (WCEN, c[t] - 2.0 * total),
                    (WCOR, 0.1 * c[t] * geo[2, t, pl.ds(r, 8), :]),
                ):
                    coef[i, k, t, pl.ds(r, 8), :] = value

    for step in range(STEPS - 1):
        @pl.loop(0, (rows + 16) // 8)
        def _(b):
            r = pl.multiple_of(OFFSET - 8 + 8 * b, 8)

            def write(f, k, t, value):
                field[(step + 1) % 2, f, k, t, pl.ds(r, 8), :] = value

            advance_block(field, coef, step % 2, r, write)

    @pl.loop(0, rows // 8)
    def _(b):
        r = pl.multiple_of(8 * b, 8)

        def write(f, k, t, value):
            if f < PR and t < 2:
                outs[f][k, pl.ds(r, 8), t * LANES : (t + 1) * LANES] = value

        advance_block(field, coef, (STEPS - 1) % 2, pl.multiple_of(OFFSET + r, 8), write)


def lon_pairs(nlon, nlat, partner):
    return [(i * nlat + j, partner(i) * nlat + j) for i in range(nlon) for j in range(nlat)]


def lat_pairs(nlon, nlat, odd):
    pairs = []
    for i in range(nlon):
        for j in range(nlat):
            up = (j % 2 == 0) != odd
            to, at = (j + 1 if up else j - 1), i
            if to < 0:
                continue
            if to == nlat:
                to, at = nlat - 1, nlon - 1 - i
            pairs.append((i * nlat + j, at * nlat + to))
    return pairs


def body(u_vel, v_vel, temp, salt, levels, land_sea, coriolis, inv_dx, inv_dy):
    args = (u_vel, v_vel, temp, salt, levels, land_sea, coriolis, inv_dx, inv_dy)
    rows, cols = levels.shape
    nlon, nlat = lax.axis_size("lon"), lax.axis_size("lat")
    axes = ("lon", "lat")
    params = pltpu.CompilerParams(vmem_limit_bytes=VMEM_LIMIT)
    f32 = jnp.float32
    column = jax.ShapeDtypeStruct((rows, LANES), f32)
    row = jax.ShapeDtypeStruct((4 * PLANES + 4, cols), f32)
    col_a, col_b, row_a, row_b = pl.pallas_call(
        pack_edges,
        in_specs=[pl.BlockSpec(memory_space=pltpu.HBM)] * 9,
        out_shape=(column, column, row, row),
        scratch_shapes=[pltpu.VMEM(a.shape, a.dtype) for a in args] + [pltpu.SemaphoreType.DMA((9,))],
        compiler_params=pltpu.CompilerParams(vmem_limit_bytes=62 * 1024 * 1024),
        name="pack_edges",
    )(*args)
    col_a = lax.ppermute(col_a, axes, lon_pairs(nlon, nlat, lambda i: i ^ 1))
    col_b = lax.ppermute(
        col_b, axes, lon_pairs(nlon, nlat, lambda i: (i + 1 if i % 2 else i - 1) % nlon)
    )
    row_a, row_b = pl.pallas_call(
        add_corners,
        out_shape=(row, row),
        compiler_params=params,
        name="add_corners",
    )(col_a, col_b, row_a, row_b)
    row_b = lax.ppermute(row_b, axes, lat_pairs(nlon, nlat, True))
    row_a = lax.ppermute(row_a, axes, lat_pairs(nlon, nlat, False))
    tall = rows + 32
    out = jax.ShapeDtypeStruct(u_vel.shape, f32)
    return pl.pallas_call(
        run_steps,
        out_shape=(out,) * 4,
        scratch_shapes=[
            pltpu.VMEM((2, 5, K, 3, tall, LANES), f32),
            pltpu.VMEM((11, K, 3, tall, LANES), f32),
            pltpu.VMEM((K, 3, tall, LANES), f32),
            pltpu.VMEM((5, 3, tall, LANES), f32),
            pltpu.VMEM((2, tall, LANES), f32),
            pltpu.VMEM(row.shape, f32),
        ],
        compiler_params=params,
        name="run_steps",
    )(*args, col_a, col_b, row_a, row_b)


def solution(mesh):
    block, plane = P(None, "lat", "lon"), P("lat", "lon")
    return jax.shard_map(
        body,
        mesh=mesh,
        in_specs=(block,) * 4 + (plane,) * 5,
        out_specs=(block,) * 4,
        check_vma=False,
    )
```

```python
import jax
import jax.numpy as jnp
from jax import lax
from jax.experimental import pallas as pl
from jax.experimental.pallas import tpu as pltpu
from jax.sharding import PartitionSpec as P

STEPS = 4
K = 3
HALO = 4
PLANES = 17
LANES = 128
OFFSET = 16
U, V, T, S, PR = range(5)
CXE, CXW, CYN, CYS, HXE, HXW, HYN, HYS, WET, WCEN, WCOR = range(11)
VMEM_LIMIT = 48 * 1024 * 1024


def plane_values(refs, p, rows, lanes):
    if p < 12:
        return refs[p // 3][p % 3, rows, lanes]
    return refs[4 + p - 12][rows, lanes].astype(jnp.float32)


def lane_index(shape):
    return lax.broadcasted_iota(jnp.int32, shape, len(shape) - 1)


def pack_columns(*refs):
    args, (out_b, out_a), ins, sems = refs[:9], refs[9:11], refs[11:20], refs[20]
    copies = [pltpu.make_async_copy(a, i, sems.at[n]) for n, (a, i) in enumerate(zip(args, ins))]
    for copy in copies:
        copy.start()
    rows, cols = ins[4].shape
    even = lax.rem(lax.axis_index("lon"), 2) == 0
    lane = lane_index((8, LANES))
    blocks = range(0, rows, 8)
    west, east = {}, {}
    for p in range(PLANES):
        if p % 3 == 0 or p > 12:
            copies[p // 3 if p < 12 else p - 8].wait()
        for r in blocks:
            w = plane_values(ins, p, slice(r, r + 8), slice(0, LANES))
            e = plane_values(ins, p, slice(r, r + 8), slice(cols - LANES, cols))
            w = pltpu.roll(w, 4 * p, 1) if p else w
            e = pltpu.roll(e, (4 * p + HALO) % LANES, 1)
            mine = lane >= 4 * p
            west[r] = jnp.where(mine, w, west[r]) if p else w
            east[r] = jnp.where(mine, e, east[r]) if p else e
    for r in blocks:
        out_a[r : r + 8, :] = jnp.where(even, east[r], west[r])
        out_b[r : r + 8, :] = jnp.where(even, west[r], east[r])


def pack_rows(*refs):
    south, north = refs[0:9], refs[9:18]
    col_b, col_a, out_b, out_a = refs[18:]
    rows = col_a.shape[0]
    even = lax.rem(lax.axis_index("lat"), 2) == 0
    for p in range(PLANES):
        s = plane_values(south, p, slice(0, 8), slice(None))[:HALO]
        n = plane_values(north, p, slice(0, 8), slice(None))[HALO:]
        out_a[4 * p : 4 * p + 4, :] = jnp.where(even, n, s)
        out_b[4 * p : 4 * p + 4, :] = jnp.where(even, s, n)
    for ref, lanes in ((col_a, slice(0, LANES)), (col_b, slice(LANES, 2 * LANES))):
        s = ref[0:HALO, :]
        n = ref[rows - HALO : rows, :]
        out_a[4 * PLANES : 4 * PLANES + 4, lanes] = jnp.where(even, n, s)
        out_b[4 * PLANES : 4 * PLANES + 4, lanes] = jnp.where(even, s, n)


def xor_rows(x, bit):
    row = lax.broadcasted_iota(jnp.int32, x.shape, 0)
    return jnp.where((row & bit) != 0, pltpu.roll(x, bit, 0), pltpu.roll(x, 8 - bit, 0))


def xor_lanes(x, bit):
    lane = lane_index(x.shape)
    if bit == LANES // 2:
        return pltpu.roll(x, bit, 1)
    return jnp.where((lane & bit) != 0, pltpu.roll(x, bit, 1), pltpu.roll(x, LANES - bit, 1))


def fold_rows(ref, out):
    lane = lane_index((8, LANES))
    row = lax.broadcasted_iota(jnp.int32, (8, LANES), 0)
    for r in range(0, 4 * PLANES + 4, 8):
        turned, short = [], []
        for t in range(2):
            x = ref[r : r + 8, t * LANES : (t + 1) * LANES]
            x = xor_rows(xor_rows(x, 1), 2)
            x = xor_lanes(xor_lanes(x, 1), 2)
            short.append(x)
            for bit in (4, 8, 16, 32, 64):
                x = xor_lanes(x, bit)
            turned.append(x)
        for t in range(2):
            x = turned[1 - t]
            if r < 24:
                x = -x
            if r + 8 > 4 * PLANES:
                packed = jnp.where(lane < 24, -short[t], short[t])
                x = jnp.where(row < 4, x, packed)
            out[r : r + 8, t * LANES : (t + 1) * LANES] = x


def shift_east(tiles, last):
    rolled = [pltpu.roll(x, LANES - 1, 1) for x in tiles]
    return [jnp.where(last, rolled[(t + 1) % 3], rolled[t]) for t in range(3)]


def shift_west(tiles, first):
    rolled = [pltpu.roll(x, 1, 1) for x in tiles]
    return [jnp.where(first, rolled[(t + 2) % 3], rolled[t]) for t in range(3)]


def density(t, s, k):
    depth = (k + 0.5) / K
    return t * ((-0.8 - 0.24 * depth) - 0.08 * t - 0.035 * s) + 0.7 * s


def advance_block(field, coef, src, r, write):
    lane = lane_index((8, LANES))
    first, last = lane == 0, lane == LANES - 1
    above = [None] * 3
    for k in range(K):
        for t in range(3):
            def get(i):
                return coef[i, k, t, pl.ds(r, 8), :]

            def fld(f, shift=0, tt=t):
                return field[src, f, k, tt, pl.ds(r + shift, 8), :]

            def around(f):
                c = fld(f)
                e = pltpu.roll(jnp.where(first, fld(f, 0, (t + 1) % 3), c), LANES - 1, 1)
                w = pltpu.roll(jnp.where(last, fld(f, 0, (t + 2) % 3), c), 1, 1)
                return c, e, w, fld(f, 1), fld(f, -1)

            cxe, cxw, cyn, cys = get(CXE), get(CXW), get(CYN), get(CYS)
            hxe, hxw, hyn, hys = get(HXE), get(HXW), get(HYN), get(HYS)
            U5, V5 = around(U), around(V)
            u, v = U5[0], V5[0]
            u2, v2 = u + u, v + v
            ae, aw = cxe - hxe * u2, cxw + hxw * u2
            an, as_ = cyn - hyn * v2, cys + hys * v2
            ac = get(WET) - ((ae + aw) + (an + as_))
            wcor = get(WCOR)
            p, pe, pw, pn, ps = around(PR)
            px = hxe * (pe - p) + hxw * (p - pw)
            py = hyn * (pn - p) + hys * (p - ps)

            def combine(X5, ac, ae, aw, an, as_):
                c, e, w, n, s = X5
                return (ac * c + (ae * e + aw * w)) + (an * n + as_ * s)

            write(U, k, t, combine(U5, ac, ae, aw, an, as_) + (wcor * v - px))
            write(V, k, t, combine(V5, ac, ae, aw, an, as_) - (wcor * u + py))
            ae = cxe - hxe * (u + U5[1])
            aw = cxw + hxw * (u + U5[2])
            an = cyn - hyn * (v + V5[3])
            as_ = cys + hys * (v + V5[4])
            ac = get(WCEN) + ((ae + aw) + (an + as_))
            t_new = combine(around(T), ac, ae, aw, an, as_)
            s_new = combine(around(S), ac, ae, aw, an, as_)
            write(T, k, t, t_new)
            write(S, k, t, s_new)
            rho = density(t_new, s_new, k)
            half = 0.5 * rho
            write(PR, k, t, half if k == 0 else above[t] + half)
            above[t] = rho if k == 0 else above[t] + rho


def run_steps(*refs):
    ins, (col_b, col_a, row_b, row_a), outs = refs[:9], refs[9:13], refs[13:17]
    field, coef, wet, geo, cols, north = refs[17:]
    rows = ins[0].shape[1]
    top = OFFSET + rows
    lon_even = lax.rem(lax.axis_index("lon"), 2) == 0
    lat = lax.axis_index("lat")
    lat_even = lax.rem(lat, 2) == 0
    lane = lane_index((8, LANES))
    first, last = lane == 0, lane == LANES - 1

    fold = lat == lax.axis_size("lat") - 1

    @pl.when(fold)
    def _():
        fold_rows(row_b, north)

    @pl.when(jnp.logical_not(fold))
    def _():
        north[...] = jnp.where(lat_even, row_a[...], row_b[...])

    def south_rows(p, lanes):
        rows_p = slice(4 * p, 4 * p + 4)
        return jnp.where(lat_even, row_b[rows_p, lanes], row_a[rows_p, lanes])

    def place(dst, a, b):
        for half, even_ref in ((0, b), (1, a)):
            odd_ref = a if half == 0 else b
            cols[half, dst, :] = jnp.where(lon_even, even_ref, odd_ref)

    place(slice(OFFSET, top), col_a[...], col_b[...])
    rows_c = slice(4 * PLANES, 4 * PLANES + 4)
    place(
        slice(OFFSET - HALO, OFFSET),
        south_rows(PLANES, slice(0, LANES)),
        south_rows(PLANES, slice(LANES, 2 * LANES)),
    )
    place(slice(top, top + HALO), north[rows_c, 0:LANES], north[rows_c, LANES : 2 * LANES])

    def target(p):
        if p < 12:
            return lambda t, dst: (field, (0, p // 3, p % 3, t, dst, slice(None)))
        return lambda t, dst: (geo, (p - 12, t, dst, slice(None)))

    for p in range(PLANES):
        at = target(p)
        for t in range(2):
            lanes = slice(t * LANES, (t + 1) * LANES)
            ref, idx = at(t, slice(OFFSET, top))
            ref[idx] = plane_values(ins, p, slice(None), lanes)
            ref, idx = at(t, slice(OFFSET - HALO, OFFSET))
            ref[idx] = south_rows(p, lanes)
            ref, idx = at(t, slice(top, top + HALO))
            ref[idx] = north[4 * p : 4 * p + 4, lanes]

    @pl.loop(0, (rows + 16) // 8)
    def _(b):
        r = pl.multiple_of(OFFSET - 8 + 8 * b, 8)
        west, east = cols[0, pl.ds(r, 8), :], cols[1, pl.ds(r, 8), :]
        for p in range(PLANES):
            e = pltpu.roll(east, LANES - 4 * p, 1) if p else east
            w = pltpu.roll(west, LANES - 4 * p - HALO, 1)
            ref, idx = target(p)(2, pl.ds(r, 8))
            ref[idx] = jnp.where(lane < LANES // 2, e, w)
        for t in range(3):
            wet_levels = jnp.where(geo[1, t, pl.ds(r, 8), :] == 1.0, geo[0, t, pl.ds(r, 8), :], 0.0)
            above = None
            for k in range(K):
                wet[k, t, pl.ds(r, 8), :] = jnp.where(wet_levels > k, 1.0, 0.0)
                rho = density(field[0, T, k, t, pl.ds(r, 8), :], field[0, S, k, t, pl.ds(r, 8), :], k)
                half = 0.5 * rho
                field[0, PR, k, t, pl.ds(r, 8), :] = half if k == 0 else above + half
                above = rho if k == 0 else above + rho

    @pl.loop(0, (rows + 16) // 8)
    def _(b):
        r = pl.multiple_of(OFFSET - 8 + 8 * b, 8)
        for k in range(K):
            c = [wet[k, t, pl.ds(r, 8), :] for t in range(3)]
            e, w = shift_east(c, last), shift_west(c, first)
            for t in range(3):
                n = wet[k, t, pl.ds(r + 1, 8), :]
                s = wet[k, t, pl.ds(r - 1, 8), :]
                idx, idy = geo[3, t, pl.ds(r, 8), :], geo[4, t, pl.ds(r, 8), :]
                hx, hy = 0.025 * idx, 0.025 * idy
                fe, fw, fn, fs = c[t] * e[t], c[t] * w[t], c[t] * n, c[t] * s
                hxe, hxw, hyn, hys = fe * hx, fw * hx, fn * hy, fs * hy
                cx, cy = 1.2 * idx, 1.2 * idy
                cxe, cxw, cyn, cys = hxe * cx, hxw * cx, hyn * cy, hys * cy
                total = (cxe + cxw) + (cyn + cys)
                for i, value in (
                    (CXE, cxe), (CXW, cxw), (CYN, cyn), (CYS, cys),
                    (HXE, hxe), (HXW, hxw), (HYN, hyn), (HYS, hys),
                    (WET, c[t]), (WCEN, c[t] - 2.0 * total),
                    (WCOR, 0.1 * c[t] * geo[2, t, pl.ds(r, 8), :]),
                ):
                    coef[i, k, t, pl.ds(r, 8), :] = value

    for step in range(STEPS - 1):
        @pl.loop(0, (rows + 16) // 8)
        def _(b):
            r = pl.multiple_of(OFFSET - 8 + 8 * b, 8)

            def write(f, k, t, value):
                field[(step + 1) % 2, f, k, t, pl.ds(r, 8), :] = value

            advance_block(field, coef, step % 2, r, write)

    @pl.loop(0, rows // 8)
    def _(b):
        r = pl.multiple_of(8 * b, 8)

        def write(f, k, t, value):
            if f < PR and t < 2:
                outs[f][k, pl.ds(r, 8), t * LANES : (t + 1) * LANES] = value

        advance_block(field, coef, (STEPS - 1) % 2, pl.multiple_of(OFFSET + r, 8), write)


def lon_pairs(nlon, nlat, partner):
    return [(i * nlat + j, partner(i) * nlat + j) for i in range(nlon) for j in range(nlat)]


def lat_pairs(nlon, nlat, odd):
    pairs = []
    for i in range(nlon):
        for j in range(nlat):
            up = (j % 2 == 0) != odd
            to, at = (j + 1 if up else j - 1), i
            if to < 0:
                continue
            if to == nlat:
                to, at = nlat - 1, nlon - 1 - i
            pairs.append((i * nlat + j, at * nlat + to))
    return pairs


def body(u_vel, v_vel, temp, salt, levels, land_sea, coriolis, inv_dx, inv_dy):
    args = (u_vel, v_vel, temp, salt, levels, land_sea, coriolis, inv_dx, inv_dy)
    rows, cols = levels.shape
    nlon, nlat = lax.axis_size("lon"), lax.axis_size("lat")
    axes = ("lon", "lat")
    params = pltpu.CompilerParams(vmem_limit_bytes=VMEM_LIMIT)
    f32 = jnp.float32
    column = jax.ShapeDtypeStruct((rows, LANES), f32)
    col_b, col_a = pl.pallas_call(
        pack_columns,
        in_specs=[pl.BlockSpec(memory_space=pltpu.HBM)] * 9,
        out_shape=(column, column),
        scratch_shapes=[pltpu.VMEM(a.shape, a.dtype) for a in args] + [pltpu.SemaphoreType.DMA((9,))],
        compiler_params=pltpu.CompilerParams(vmem_limit_bytes=62 * 1024 * 1024),
        name="pack_columns",
    )(*args)
    col_b = lax.ppermute(
        col_b, axes, lon_pairs(nlon, nlat, lambda i: (i + 1 if i % 2 else i - 1) % nlon)
    )
    col_a = lax.ppermute(col_a, axes, lon_pairs(nlon, nlat, lambda i: i ^ 1))

    def edge(block):
        def spec(a):
            if a.ndim == 3:
                return pl.BlockSpec((K, 8, cols), lambda i: (0, block, 0))
            return pl.BlockSpec((8, cols), lambda i: (block, 0))
        return [spec(a) for a in args]

    whole = pl.BlockSpec((rows, LANES), lambda i: (0, 0))
    row = jax.ShapeDtypeStruct((4 * PLANES + 4, cols), f32)
    row_spec = pl.BlockSpec(row.shape, lambda i: (0, 0))
    row_b, row_a = pl.pallas_call(
        pack_rows,
        grid=(1,),
        in_specs=edge(0) + edge(rows // 8 - 1) + [whole, whole],
        out_specs=(row_spec, row_spec),
        out_shape=(row, row),
        compiler_params=params,
        name="pack_rows",
    )(*args, *args, col_b, col_a)
    row_b = lax.ppermute(row_b, axes, lat_pairs(nlon, nlat, True))
    row_a = lax.ppermute(row_a, axes, lat_pairs(nlon, nlat, False))
    tall = rows + 32
    out = jax.ShapeDtypeStruct(u_vel.shape, f32)
    return pl.pallas_call(
        run_steps,
        out_shape=(out,) * 4,
        scratch_shapes=[
            pltpu.VMEM((2, 5, K, 3, tall, LANES), f32),
            pltpu.VMEM((11, K, 3, tall, LANES), f32),
            pltpu.VMEM((K, 3, tall, LANES), f32),
            pltpu.VMEM((5, 3, tall, LANES), f32),
            pltpu.VMEM((2, tall, LANES), f32),
            pltpu.VMEM(row.shape, f32),
        ],
        compiler_params=params,
        name="run_steps",
    )(*args, col_b, col_a, row_b, row_a)


def solution(mesh):
    block, plane = P(None, "lat", "lon"), P("lat", "lon")
    return jax.shard_map(
        body,
        mesh=mesh,
        in_specs=(block,) * 4 + (plane,) * 5,
        out_specs=(block,) * 4,
        check_vma=False,
    )
```

```python
import jax
import jax.numpy as jnp
from jax import lax
from jax.experimental import pallas as pl
from jax.experimental.pallas import tpu as pltpu
from jax.sharding import PartitionSpec as P

STEPS = 4
K = 3
HALO = 4
PLANES = 17
LANES = 128
OFFSET = 16
U, V, T, S, PR = range(5)
CXE, CXW, CYN, CYS, HXE, HXW, HYN, HYS, WET, WCEN, WCOR = range(11)
VMEM_LIMIT = 28 * 1024 * 1024


def plane_values(refs, p, rows, lanes):
    if p < 12:
        return refs[p // 3][p % 3, rows, lanes]
    return refs[4 + p - 12][rows, lanes].astype(jnp.float32)


def lane_index(shape):
    return lax.broadcasted_iota(jnp.int32, shape, len(shape) - 1)


def pack_columns(*refs):
    args, (out_b, out_a), ins, sems = refs[:9], refs[9:11], refs[11:20], refs[20]
    copies = [pltpu.make_async_copy(a, i, sems.at[n]) for n, (a, i) in enumerate(zip(args, ins))]
    for copy in copies:
        copy.start()
    rows, cols = ins[4].shape
    even = lax.rem(lax.axis_index("lon"), 2) == 0
    lane = lane_index((8, LANES))
    blocks = range(0, rows, 8)
    west, east = {}, {}
    for p in range(PLANES):
        if p % 3 == 0 or p > 12:
            copies[p // 3 if p < 12 else p - 8].wait()
        for r in blocks:
            w = plane_values(ins, p, slice(r, r + 8), slice(0, LANES))
            e = plane_values(ins, p, slice(r, r + 8), slice(cols - LANES, cols))
            w = pltpu.roll(w, 4 * p, 1) if p else w
            e = pltpu.roll(e, (4 * p + HALO) % LANES, 1)
            mine = lane >= 4 * p
            west[r] = jnp.where(mine, w, west[r]) if p else w
            east[r] = jnp.where(mine, e, east[r]) if p else e
    for r in blocks:
        out_a[r : r + 8, :] = jnp.where(even, east[r], west[r])
        out_b[r : r + 8, :] = jnp.where(even, west[r], east[r])


def pack_rows(*refs):
    south, north = refs[0:9], refs[9:18]
    col_b, col_a, out_b, out_a = refs[18:]
    rows = col_a.shape[0]
    even = lax.rem(lax.axis_index("lat"), 2) == 0
    for p in range(PLANES):
        s = plane_values(south, p, slice(0, 8), slice(None))[:HALO]
        n = plane_values(north, p, slice(0, 8), slice(None))[HALO:]
        out_a[4 * p : 4 * p + 4, :] = jnp.where(even, n, s)
        out_b[4 * p : 4 * p + 4, :] = jnp.where(even, s, n)
    for ref, lanes in ((col_a, slice(0, LANES)), (col_b, slice(LANES, 2 * LANES))):
        s = ref[0:HALO, :]
        n = ref[rows - HALO : rows, :]
        out_a[4 * PLANES : 4 * PLANES + 4, lanes] = jnp.where(even, n, s)
        out_b[4 * PLANES : 4 * PLANES + 4, lanes] = jnp.where(even, s, n)


def xor_rows(x, bit):
    row = lax.broadcasted_iota(jnp.int32, x.shape, 0)
    return jnp.where((row & bit) != 0, pltpu.roll(x, bit, 0), pltpu.roll(x, 8 - bit, 0))


def xor_lanes(x, bit):
    lane = lane_index(x.shape)
    if bit == LANES // 2:
        return pltpu.roll(x, bit, 1)
    return jnp.where((lane & bit) != 0, pltpu.roll(x, bit, 1), pltpu.roll(x, LANES - bit, 1))


def fold_rows(ref, out):
    lane = lane_index((8, LANES))
    row = lax.broadcasted_iota(jnp.int32, (8, LANES), 0)
    for r in range(0, 4 * PLANES + 4, 8):
        turned, short = [], []
        for t in range(2):
            x = ref[r : r + 8, t * LANES : (t + 1) * LANES]
            x = xor_rows(xor_rows(x, 1), 2)
            x = xor_lanes(xor_lanes(x, 1), 2)
            short.append(x)
            for bit in (4, 8, 16, 32, 64):
                x = xor_lanes(x, bit)
            turned.append(x)
        for t in range(2):
            x = turned[1 - t]
            if r < 24:
                x = -x
            if r + 8 > 4 * PLANES:
                packed = jnp.where(lane < 24, -short[t], short[t])
                x = jnp.where(row < 4, x, packed)
            out[r : r + 8, t * LANES : (t + 1) * LANES] = x


def density(t, s, slope):
    return t * (slope - 0.08 * t - 0.035 * s) + 0.7 * s


def slope_of(level):
    return -0.8 - 0.24 * ((level + 0.5) / K)


def column_pressure(rhos):
    above, out = None, []
    for rho in rhos:
        half = 0.5 * rho
        out.append(half if above is None else above + half)
        above = rho if above is None else above + rho
    return out


def coefficients(c, e, w, n, s, coriolis, idx, idy):
    hx, hy = 0.025 * idx, 0.025 * idy
    hxe, hxw, hyn, hys = c * e * hx, c * w * hx, c * n * hy, c * s * hy
    cx, cy = 1.2 * idx, 1.2 * idy
    cxe, cxw, cyn, cys = hxe * cx, hxw * cx, hyn * cy, hys * cy
    total = (cxe + cxw) + (cyn + cys)
    return cxe, cxw, cyn, cys, hxe, hxw, hyn, hys, c, c - 2.0 * total, 0.1 * c * coriolis


def advance(around, get):
    cxe, cxw, cyn, cys = get(CXE), get(CXW), get(CYN), get(CYS)
    hxe, hxw, hyn, hys = get(HXE), get(HXW), get(HYN), get(HYS)
    us, vs = around(U), around(V)
    u, v = us[0], vs[0]
    u2, v2 = u + u, v + v
    ae, aw = cxe - hxe * u2, cxw + hxw * u2
    an, as_ = cyn - hyn * v2, cys + hys * v2
    ac = get(WET) - ((ae + aw) + (an + as_))
    wcor = get(WCOR)
    p, pe, pw, pn, ps = around(PR)
    px = hxe * (pe - p) + hxw * (p - pw)
    py = hyn * (pn - p) + hys * (p - ps)

    def combine(xs, ac, ae, aw, an, as_):
        c, e, w, n, s = xs
        return (ac * c + (ae * e + aw * w)) + (an * n + as_ * s)

    u_new = combine(us, ac, ae, aw, an, as_) + (wcor * v - px)
    v_new = combine(vs, ac, ae, aw, an, as_) - (wcor * u + py)
    ae = cxe - hxe * (u + us[1])
    aw = cxw + hxw * (u + us[2])
    an = cyn - hyn * (v + vs[3])
    as_ = cys + hys * (v + vs[4])
    ac = get(WCEN) + ((ae + aw) + (an + as_))
    t_new = combine(around(T), ac, ae, aw, an, as_)
    s_new = combine(around(S), ac, ae, aw, an, as_)
    return u_new, v_new, t_new, s_new


def east_west(c, other, t):
    lane = lane_index(c.shape)
    if t == 0:
        e = pltpu.roll(jnp.where(lane == 0, other, c), LANES - 1, 1)
        w = pltpu.roll(c, 1, 1)
    else:
        e = pltpu.roll(c, LANES - 1, 1)
        w = pltpu.roll(jnp.where(lane == LANES - 1, other, c), 1, 1)
    return e, w


def advance_tiles(field, coef, r, write, last=False):
    for t in range(2):
        above = None
        for k in range(K):
            def around(f):
                c = field(f, k, t, r)
                e, w = east_west(c, field(f, k, 1 - t, r), t)
                return c, e, w, field(f, k, t, r + 1), field(f, k, t, r - 1)

            new = advance(around, lambda i: coef(i, k, t, r))
            for f in range(4):
                write(f, k, t, new[f])
            if not last:
                rho = density(new[T], new[S], slope_of(k))
                half = 0.5 * rho
                write(PR, k, t, half if k == 0 else above + half)
                above = rho if k == 0 else above + rho


def tile_coefficients(wet, geo, r, write):
    for k in range(K):
        for t in range(2):
            c = wet(k, t, r)
            e, w = east_west(c, wet(k, 1 - t, r), t)
            values = coefficients(
                c, e, w, wet(k, t, r + 1), wet(k, t, r - 1), geo(0, t, r), geo(1, t, r), geo(2, t, r)
            )
            for i, value in enumerate(values):
                write(i, k, t, value)


def strip_of(tiles):
    lane = lane_index((8, LANES))
    out = None
    for k, (low, high) in enumerate(tiles):
        x = pltpu.roll(low, 32 * k + 4, 1)
        y = pltpu.roll(high, (32 * k - 100) % LANES, 1)
        both = jnp.where(lane >= 32 * k + 16, y, x)
        out = both if k == 0 else jnp.where(lane >= 32 * k, both, out)
    return out


def run_interior(*refs):
    ins, states, outs, strip = refs[:9], refs[10:14], refs[14:18], refs[18]
    coef, wet = refs[19:]
    rows = ins[4].shape[0]
    tiles = [slice(t * LANES, (t + 1) * LANES) for t in range(2)]

    @pl.loop(0, rows // 8)
    def _(b):
        q = pl.multiple_of(8 * b, 8)
        r = pl.multiple_of(8 * b + 8, 8)
        at, own = pl.ds(r, 8), pl.ds(q, 8)
        for f in range(4):
            for k in range(K):
                for t in range(2):
                    states[0][f, k, t, at, :] = ins[f][k, own, tiles[t]]
            strip[f, own, :] = strip_of([[ins[f][k, own, tiles[t]] for t in range(2)] for k in range(K)])
        for i in range(5):
            strip[4 + i, own, :] = strip_of([[ins[4 + i][own, tiles[t]].astype(jnp.float32) for t in range(2)]] * K)
        for t in range(2):
            sea = ins[5][own, tiles[t]] == 1
            rhos = []
            for k in range(K):
                wet[k, t, at, :] = jnp.where(sea & (ins[4][own, tiles[t]] > k), 1.0, 0.0)
                rhos.append(density(ins[T][k, own, tiles[t]], ins[S][k, own, tiles[t]], slope_of(k)))
            for k, value in enumerate(column_pressure(rhos)):
                states[0][PR, k, t, at, :] = value

    @pl.loop(0, rows // 8)
    def _(b):
        r = pl.multiple_of(8 * b + 8, 8)

        def write(i, k, t, value):
            coef[i, k, t, pl.ds(r, 8), :] = value

        tile_coefficients(
            lambda k, t, row: wet[k, t, pl.ds(row, 8), :],
            lambda i, t, row: ins[6 + i][pl.ds(pl.multiple_of(8 * b, 8), 8), tiles[t]],
            r,
            write,
        )

    for step in range(STEPS):
        @pl.loop(0, rows // 8)
        def _(b):
            r = pl.multiple_of(8 * b + 8, 8)

            def write(f, k, t, value):
                if step < STEPS - 1:
                    states[step + 1][f, k, t, pl.ds(r, 8), :] = value
                else:
                    outs[f][k, pl.ds(pl.multiple_of(8 * b, 8), 8), tiles[t]] = value

            advance_tiles(
                lambda f, k, t, row: states[step][f, k, t, pl.ds(row, 8), :],
                lambda i, k, t, row: coef[i, k, t, pl.ds(row, 8), :],
                r,
                write,
                last=step == STEPS - 1,
            )


def run_rims(*refs):
    geo_in, states, parts, strip_in = refs[0:5], refs[5:9], refs[9:13], refs[13]
    col_b, col_a, row_b, row_a = refs[14:18]
    outs = refs[18:22]
    north, cols, band, band_geo, band_wet, band_coef, sf, sg, sw, sc = refs[22:]
    rows = geo_in[0].shape[0]
    top = OFFSET + rows
    lon_even = lax.rem(lax.axis_index("lon"), 2) == 0
    lat = lax.axis_index("lat")
    lat_even = lax.rem(lat, 2) == 0
    lane = lane_index((8, LANES))
    tiles = [slice(t * LANES, (t + 1) * LANES) for t in range(2)]
    fold = lat == lax.axis_size("lat") - 1

    @pl.when(fold)
    def _():
        fold_rows(row_b, north)

    @pl.when(jnp.logical_not(fold))
    def _():
        north[...] = jnp.where(lat_even, row_a[...], row_b[...])

    def south_rows(p, lanes):
        rows_p = slice(4 * p, 4 * p + 4)
        return jnp.where(lat_even, row_b[rows_p, lanes], row_a[rows_p, lanes])

    def north_rows(p, lanes):
        return north[4 * p : 4 * p + 4, lanes]

    def place(dst, a, b):
        cols[0, dst, :] = jnp.where(lon_even, b, a)
        cols[1, dst, :] = jnp.where(lon_even, a, b)

    place(slice(OFFSET, top), col_a[...], col_b[...])
    place(slice(OFFSET - HALO, OFFSET), *(south_rows(PLANES, tiles[i]) for i in range(2)))
    place(slice(top, top + HALO), *(north_rows(PLANES, tiles[i]) for i in range(2)))

    own = ((16, 0), (8, rows - 16))
    far = ((24, 8), (8, rows - 16))
    halo = ((12, south_rows), (24, north_rows))
    blocks = ((8, 16), (16, 24))
    for side in range(2):
        put, first = own[side]
        place_h, rows_of = halo[side]
        for t in range(2):
            for f in range(4):
                for k in range(K):
                    band[side, 0, f, k, t, place_h : place_h + 4, :] = rows_of(3 * f + k, tiles[t])
            for i in range(5):
                band_geo[side, i, t, put : put + 16, :] = geo_in[i][first : first + 16, tiles[t]].astype(jnp.float32)
                band_geo[side, i, t, place_h : place_h + 4, :] = rows_of(12 + i, tiles[t])
            for k in range(K):
                for f in range(5):
                    band[side, 0, f, k, t, put : put + 16, :] = states[0][f, k, t, first + 8 : first + 24, :]
                    for step in range(1, STEPS):
                        at, start = far[side]
                        band[side, step, f, k, t, at : at + 8, :] = states[step][f, k, t, start + 8 : start + 16, :]
            at = 8 if side == 0 else 24
            rhos = [
                density(band[side, 0, T, k, t, at : at + 8, :], band[side, 0, S, k, t, at : at + 8, :], slope_of(k))
                for k in range(K)
            ]
            for k, value in enumerate(column_pressure(rhos)):
                band[side, 0, PR, k, t, at : at + 8, :] = value
            for at in (8, 16, 24):
                sea = band_geo[side, 1, t, at : at + 8, :] == 1.0
                for k in range(K):
                    wet = sea & (band_geo[side, 0, t, at : at + 8, :] > k)
                    band_wet[side, k, t, at : at + 8, :] = jnp.where(wet, 1.0, 0.0)

    own_rows = slice(OFFSET, top)
    for f in range(4):
        sf[0, f, own_rows, :] = strip_in[f]
    for i in range(5):
        sg[i, own_rows, :] = strip_in[4 + i]
    for side, (at, to) in enumerate(((8, OFFSET - 8), (24, top))):
        for f in range(4):
            sf[0, f, to : to + 8, :] = strip_of(
                [[band[side, 0, f, k, t, at : at + 8, :] for t in range(2)] for k in range(K)]
            )
        for i in range(5):
            sg[i, to : to + 8, :] = strip_of([[band_geo[side, i, t, at : at + 8, :] for t in range(2)]] * K)
    level = lane // 32
    slope = slope_of(level.astype(jnp.float32))

    def strip_pressure(t, s):
        rho = density(t, s, slope)
        one = jnp.where(lane >= 32, pltpu.roll(rho, 32, 1), 0.0)
        two = jnp.where(lane >= 64, pltpu.roll(rho, 64, 1), 0.0)
        return 0.5 * rho + (one + two)

    @pl.loop(0, (rows + 16) // 8)
    def _(b):
        r = pl.multiple_of(OFFSET - 8 + 8 * b, 8)
        at = pl.ds(r, 8)
        west, east = cols[0, at, :], cols[1, at, :]

        def insert(x, planes):
            for k, p in enumerate(planes):
                w = pltpu.roll(west, (32 * k - 4 * p) % LANES, 1)
                e = pltpu.roll(east, (32 * k + 28 - 4 * p) % LANES, 1)
                x = jnp.where((lane >= 32 * k) & (lane < 32 * k + 4), w, x)
                x = jnp.where((lane >= 32 * k + 28) & (lane < 32 * k + 32), e, x)
            return x

        for f in range(4):
            sf[0, f, at, :] = insert(sf[0, f, at, :], (3 * f, 3 * f + 1, 3 * f + 2))
        for i in range(5):
            sg[i, at, :] = insert(sg[i, at, :], (12 + i,) * K)
        sf[0, PR, at, :] = strip_pressure(sf[0, T, at, :], sf[0, S, at, :])
        wet = (sg[1, at, :] == 1.0) & (sg[0, at, :] > level.astype(jnp.float32))
        sw[at, :] = jnp.where(wet, 1.0, 0.0)

    def rolled(c):
        return pltpu.roll(c, LANES - 1, 1), pltpu.roll(c, 1, 1)

    @pl.loop(0, (rows + 16) // 8)
    def _(b):
        r = pl.multiple_of(OFFSET - 8 + 8 * b, 8)
        at = pl.ds(r, 8)
        c = sw[at, :]
        e, w = rolled(c)
        values = coefficients(
            c, e, w, sw[pl.ds(r + 1, 8), :], sw[pl.ds(r - 1, 8), :], sg[2, at, :], sg[3, at, :], sg[4, at, :]
        )
        for i, value in enumerate(values):
            sc[i, at, :] = value

    for side in range(2):
        @pl.loop(0, 2)
        def _(b):
            r = pl.multiple_of(blocks[side][0] + 8 * b, 8)

            def write(i, k, t, value):
                band_coef[side, i, k, t, pl.ds(r, 8), :] = value

            tile_coefficients(
                lambda k, t, row: band_wet[side, k, t, pl.ds(row, 8), :],
                lambda i, t, row: band_geo[side, 2 + i, t, pl.ds(row, 8), :],
                r,
                write,
            )

    for step in range(STEPS):
        final = step == STEPS - 1

        @pl.loop(0, 2 if final else 4)
        def _(n):
            side = n if final else lax.div(n, 2)
            r = pl.multiple_of(16 + 0 * n if final else 8 + 8 * (lax.rem(n, 2) + side), 8)

            def write(f, k, t, value):
                if final:
                    to = pl.multiple_of(side * (rows - 8), 8)
                    outs[f][k, pl.ds(to, 8), tiles[t]] = value
                else:
                    band[side, step + 1, f, k, t, pl.ds(r, 8), :] = value

            advance_tiles(
                lambda f, k, t, row: band[side, step, f, k, t, pl.ds(row, 8), :],
                lambda i, k, t, row: band_coef[side, i, k, t, pl.ds(row, 8), :],
                r,
                write,
                last=final,
            )

    def strip_step(step, r):
        at = pl.ds(r, 8)

        def around(f):
            c = sf[step % 2, f, at, :]
            return (c,) + rolled(c) + (sf[step % 2, f, pl.ds(r + 1, 8), :], sf[step % 2, f, pl.ds(r - 1, 8), :])

        return advance(around, lambda i: sc[i, at, :])

    for step in range(STEPS - 1):
        @pl.loop(0, (rows + 16) // 8)
        def _(b):
            r = pl.multiple_of(OFFSET - 8 + 8 * b, 8)
            new = strip_step(step, r)
            for f in range(4):
                sf[(step + 1) % 2, f, pl.ds(r, 8), :] = new[f]
            sf[(step + 1) % 2, PR, pl.ds(r, 8), :] = strip_pressure(new[T], new[S])

    def finish(q, source):
        new = strip_step(STEPS - 1, q + OFFSET)
        at = pl.ds(q, 8)
        for f in range(4):
            for k in range(K):
                low = pltpu.roll(new[f], (-32 * k - 4) % LANES, 1)
                high = pltpu.roll(new[f], 100 - 32 * k, 1)
                outs[f][k, at, tiles[0]] = jnp.where(lane < HALO, low, source[f][k, at, tiles[0]])
                outs[f][k, at, tiles[1]] = jnp.where(lane >= LANES - HALO, high, source[f][k, at, tiles[1]])

    finish(0, outs)
    finish(rows - 8, outs)

    @pl.loop(1, rows // 8 - 1)
    def _(b):
        finish(pl.multiple_of(8 * b, 8), parts)


def lon_pairs(nlon, nlat, partner):
    return [(i * nlat + j, partner(i) * nlat + j) for i in range(nlon) for j in range(nlat)]


def lat_pairs(nlon, nlat, odd):
    pairs = []
    for i in range(nlon):
        for j in range(nlat):
            up = (j % 2 == 0) != odd
            to, at = (j + 1 if up else j - 1), i
            if to < 0:
                continue
            if to == nlat:
                to, at = nlat - 1, nlon - 1 - i
            pairs.append((i * nlat + j, at * nlat + to))
    return pairs


def body(u_vel, v_vel, temp, salt, levels, land_sea, coriolis, inv_dx, inv_dy):
    args = (u_vel, v_vel, temp, salt, levels, land_sea, coriolis, inv_dx, inv_dy)
    rows, cols = levels.shape
    nlon, nlat = lax.axis_size("lon"), lax.axis_size("lat")
    axes = ("lon", "lat")
    params = pltpu.CompilerParams(vmem_limit_bytes=VMEM_LIMIT)
    f32 = jnp.float32
    column = jax.ShapeDtypeStruct((rows, LANES), f32)
    col_b, col_a = pl.pallas_call(
        pack_columns,
        in_specs=[pl.BlockSpec(memory_space=pltpu.HBM)] * 9,
        out_shape=(column, column),
        scratch_shapes=[pltpu.VMEM(a.shape, a.dtype) for a in args] + [pltpu.SemaphoreType.DMA((9,))],
        compiler_params=pltpu.CompilerParams(vmem_limit_bytes=62 * 1024 * 1024),
        name="pack_columns",
    )(*args)
    col_b = lax.ppermute(
        col_b, axes, lon_pairs(nlon, nlat, lambda i: (i + 1 if i % 2 else i - 1) % nlon)
    )
    col_a = lax.ppermute(col_a, axes, lon_pairs(nlon, nlat, lambda i: i ^ 1))

    def edge(block):
        def spec(a):
            if a.ndim == 3:
                return pl.BlockSpec((K, 8, cols), lambda i: (0, block, 0))
            return pl.BlockSpec((8, cols), lambda i: (block, 0))
        return [spec(a) for a in args]

    whole = pl.BlockSpec((rows, LANES), lambda i: (0, 0))
    row = jax.ShapeDtypeStruct((4 * PLANES + 4, cols), f32)
    row_spec = pl.BlockSpec(row.shape, lambda i: (0, 0))
    row_b, row_a = pl.pallas_call(
        pack_rows,
        grid=(1,),
        in_specs=edge(0) + edge(rows // 8 - 1) + [whole, whole],
        out_specs=(row_spec, row_spec),
        out_shape=(row, row),
        compiler_params=params,
        name="pack_rows",
    )(*args, *args, col_b, col_a)
    sent = row_a
    row_b = lax.ppermute(row_b, axes, lat_pairs(nlon, nlat, True))
    row_a = lax.ppermute(row_a, axes, lat_pairs(nlon, nlat, False))
    out = jax.ShapeDtypeStruct(u_vel.shape, f32)
    state = jax.ShapeDtypeStruct((5, K, 2, rows + 16, LANES), f32)
    vmem = pl.BlockSpec(memory_space=pltpu.VMEM)
    *kept, strip = pl.pallas_call(
        run_interior,
        in_specs=[vmem] * 9 + [pl.BlockSpec(memory_space=pl.ANY)],
        out_shape=(state,) * 4 + (out,) * 4 + (jax.ShapeDtypeStruct((9, rows, LANES), f32),),
        scratch_shapes=[
            pltpu.VMEM((11, K, 2, rows + 16, LANES), f32),
            pltpu.VMEM((K, 2, rows + 16, LANES), f32),
        ],
        compiler_params=params,
        cost_estimate=pl.CostEstimate(flops=30_000_000, bytes_accessed=16_000_000, transcendentals=0),
        name="run_interior",
    )(*args, sent)
    tall = rows + 32
    return pl.pallas_call(
        run_rims,
        out_shape=(out,) * 4,
        scratch_shapes=[
            pltpu.VMEM(row.shape, f32),
            pltpu.VMEM((2, tall, LANES), f32),
            pltpu.VMEM((2, 4, 5, K, 2, 40, LANES), f32),
            pltpu.VMEM((2, 5, 2, 40, LANES), f32),
            pltpu.VMEM((2, K, 2, 40, LANES), f32),
            pltpu.VMEM((2, 11, K, 2, 40, LANES), f32),
            pltpu.VMEM((2, 5, tall, LANES), f32),
            pltpu.VMEM((5, tall, LANES), f32),
            pltpu.VMEM((tall, LANES), f32),
            pltpu.VMEM((11, tall, LANES), f32),
        ],
        compiler_params=params,
        name="run_rims",
    )(*args[4:], *kept, strip, col_b, col_a, row_b, row_a)


def solution(mesh):
    block, plane = P(None, "lat", "lon"), P("lat", "lon")
    return jax.shard_map(
        body,
        mesh=mesh,
        in_specs=(block,) * 4 + (plane,) * 5,
        out_specs=(block,) * 4,
        check_vma=False,
    )
```

```python
import jax
import jax.numpy as jnp
from jax import lax
from jax.experimental import pallas as pl
from jax.experimental.pallas import tpu as pltpu
from jax.sharding import PartitionSpec as P

STEPS = 4
K = 3
HALO = 4
PLANES = 17
LANES = 128
OFFSET = 16
U, V, T, S, PR = range(5)
CXE, CXW, CYN, CYS, HXE, HXW, HYN, HYS, WET, WCEN, WCOR = range(11)
VMEM_LIMIT = 28 * 1024 * 1024


def plane_values(refs, p, rows, lanes):
    if p < 12:
        return refs[p // 3][p % 3, rows, lanes]
    return refs[4 + p - 12][rows, lanes].astype(jnp.float32)


def lane_index(shape):
    return lax.broadcasted_iota(jnp.int32, shape, len(shape) - 1)


def pack_columns(*refs):
    args, (out_b, out_a), ins, sems = refs[:9], refs[9:11], refs[11:20], refs[20]
    copies = [pltpu.make_async_copy(a, i, sems.at[n]) for n, (a, i) in enumerate(zip(args, ins))]
    for copy in copies:
        copy.start()
    rows, cols = ins[4].shape
    even = lax.rem(lax.axis_index("lon"), 2) == 0
    lane = lane_index((8, LANES))
    blocks = range(0, rows, 8)
    west, east = {}, {}
    for p in range(PLANES):
        if p % 3 == 0 or p > 12:
            copies[p // 3 if p < 12 else p - 8].wait()
        for r in blocks:
            w = plane_values(ins, p, slice(r, r + 8), slice(0, LANES))
            e = plane_values(ins, p, slice(r, r + 8), slice(cols - LANES, cols))
            w = pltpu.roll(w, 4 * p, 1) if p else w
            e = pltpu.roll(e, (4 * p + HALO) % LANES, 1)
            mine = lane >= 4 * p
            west[r] = jnp.where(mine, w, west[r]) if p else w
            east[r] = jnp.where(mine, e, east[r]) if p else e
    for r in blocks:
        out_a[r : r + 8, :] = jnp.where(even, east[r], west[r])
        out_b[r : r + 8, :] = jnp.where(even, west[r], east[r])


def pack_rows(*refs):
    south, north = refs[0:9], refs[9:18]
    col_b, col_a, out_b, out_a = refs[18:]
    rows = col_a.shape[0]
    even = lax.rem(lax.axis_index("lat"), 2) == 0
    for p in range(PLANES):
        s = plane_values(south, p, slice(0, 8), slice(None))[:HALO]
        n = plane_values(north, p, slice(0, 8), slice(None))[HALO:]
        out_a[4 * p : 4 * p + 4, :] = jnp.where(even, n, s)
        out_b[4 * p : 4 * p + 4, :] = jnp.where(even, s, n)
    for ref, lanes in ((col_a, slice(0, LANES)), (col_b, slice(LANES, 2 * LANES))):
        s = ref[0:HALO, :]
        n = ref[rows - HALO : rows, :]
        out_a[4 * PLANES : 4 * PLANES + 4, lanes] = jnp.where(even, n, s)
        out_b[4 * PLANES : 4 * PLANES + 4, lanes] = jnp.where(even, s, n)


def xor_rows(x, bit):
    row = lax.broadcasted_iota(jnp.int32, x.shape, 0)
    return jnp.where((row & bit) != 0, pltpu.roll(x, bit, 0), pltpu.roll(x, 8 - bit, 0))


def xor_lanes(x, bit):
    lane = lane_index(x.shape)
    if bit == LANES // 2:
        return pltpu.roll(x, bit, 1)
    return jnp.where((lane & bit) != 0, pltpu.roll(x, bit, 1), pltpu.roll(x, LANES - bit, 1))


def fold_rows(ref, out):
    lane = lane_index((8, LANES))
    row = lax.broadcasted_iota(jnp.int32, (8, LANES), 0)
    for r in range(0, 4 * PLANES + 4, 8):
        turned, short = [], []
        for t in range(2):
            x = ref[r : r + 8, t * LANES : (t + 1) * LANES]
            x = xor_rows(xor_rows(x, 1), 2)
            x = xor_lanes(xor_lanes(x, 1), 2)
            short.append(x)
            for bit in (4, 8, 16, 32, 64):
                x = xor_lanes(x, bit)
            turned.append(x)
        for t in range(2):
            x = turned[1 - t]
            if r < 24:
                x = -x
            if r + 8 > 4 * PLANES:
                packed = jnp.where(lane < 24, -short[t], short[t])
                x = jnp.where(row < 4, x, packed)
            out[r : r + 8, t * LANES : (t + 1) * LANES] = x


def density(t, s, slope):
    return t * (slope - 0.08 * t - 0.035 * s) + 0.7 * s


def slope_of(level):
    return -0.8 - 0.24 * ((level + 0.5) / K)


def column_pressure(rhos):
    above, out = None, []
    for rho in rhos:
        half = 0.5 * rho
        out.append(half if above is None else above + half)
        above = rho if above is None else above + rho
    return out


def coefficients(c, e, w, n, s, coriolis, idx, idy):
    hx, hy = 0.025 * idx, 0.025 * idy
    hxe, hxw, hyn, hys = c * e * hx, c * w * hx, c * n * hy, c * s * hy
    cx, cy = 1.2 * idx, 1.2 * idy
    cxe, cxw, cyn, cys = hxe * cx, hxw * cx, hyn * cy, hys * cy
    total = (cxe + cxw) + (cyn + cys)
    return cxe, cxw, cyn, cys, hxe, hxw, hyn, hys, c, c - 2.0 * total, 0.1 * c * coriolis


def advance(around, get):
    cxe, cxw, cyn, cys = get(CXE), get(CXW), get(CYN), get(CYS)
    hxe, hxw, hyn, hys = get(HXE), get(HXW), get(HYN), get(HYS)
    us, vs = around(U), around(V)
    u, v = us[0], vs[0]
    u2, v2 = u + u, v + v
    ae, aw = cxe - hxe * u2, cxw + hxw * u2
    an, as_ = cyn - hyn * v2, cys + hys * v2
    ac = get(WET) - ((ae + aw) + (an + as_))
    wcor = get(WCOR)
    p, pe, pw, pn, ps = around(PR)
    px = hxe * (pe - p) + hxw * (p - pw)
    py = hyn * (pn - p) + hys * (p - ps)

    def combine(xs, ac, ae, aw, an, as_):
        c, e, w, n, s = xs
        return (ac * c + (ae * e + aw * w)) + (an * n + as_ * s)

    u_new = combine(us, ac, ae, aw, an, as_) + (wcor * v - px)
    v_new = combine(vs, ac, ae, aw, an, as_) - (wcor * u + py)
    ae = cxe - hxe * (u + us[1])
    aw = cxw + hxw * (u + us[2])
    an = cyn - hyn * (v + vs[3])
    as_ = cys + hys * (v + vs[4])
    ac = get(WCEN) + ((ae + aw) + (an + as_))
    t_new = combine(around(T), ac, ae, aw, an, as_)
    s_new = combine(around(S), ac, ae, aw, an, as_)
    return u_new, v_new, t_new, s_new


def east_west(c, other, t):
    lane = lane_index(c.shape)
    if t == 0:
        e = pltpu.roll(jnp.where(lane == 0, other, c), LANES - 1, 1)
        w = pltpu.roll(c, 1, 1)
    else:
        e = pltpu.roll(c, LANES - 1, 1)
        w = pltpu.roll(jnp.where(lane == LANES - 1, other, c), 1, 1)
    return e, w


def advance_tiles(field, coef, r, write, last=False):
    for t in range(2):
        above = None
        for k in range(K):
            def around(f):
                c = field(f, k, t, r)
                e, w = east_west(c, field(f, k, 1 - t, r), t)
                return c, e, w, field(f, k, t, r + 1), field(f, k, t, r - 1)

            new = advance(around, lambda i: coef(i, k, t, r))
            for f in range(4):
                write(f, k, t, new[f])
            if not last:
                rho = density(new[T], new[S], slope_of(k))
                half = 0.5 * rho
                write(PR, k, t, half if k == 0 else above + half)
                above = rho if k == 0 else above + rho


def tile_coefficients(wet, geo, r, write):
    for k in range(K):
        for t in range(2):
            c = wet(k, t, r)
            e, w = east_west(c, wet(k, 1 - t, r), t)
            values = coefficients(
                c, e, w, wet(k, t, r + 1), wet(k, t, r - 1), geo(0, t, r), geo(1, t, r), geo(2, t, r)
            )
            for i, value in enumerate(values):
                write(i, k, t, value)


def strip_of(tiles):
    lane = lane_index((8, LANES))
    out = None
    for k, (low, high) in enumerate(tiles):
        x = pltpu.roll(low, 32 * k + 4, 1)
        y = pltpu.roll(high, (32 * k - 100) % LANES, 1)
        both = jnp.where(lane >= 32 * k + 16, y, x)
        out = both if k == 0 else jnp.where(lane >= 32 * k, both, out)
    return out


def run_interior(*refs):
    ins, states, outs, strip = refs[:9], refs[10:14], refs[14:18], refs[18]
    coef, wet = refs[19:]
    rows = ins[4].shape[0]
    tiles = [slice(t * LANES, (t + 1) * LANES) for t in range(2)]

    @pl.loop(0, rows // 8, unroll=6)
    def _(b):
        q = pl.multiple_of(8 * b, 8)
        r = pl.multiple_of(8 * b + 8, 8)
        at, own = pl.ds(r, 8), pl.ds(q, 8)
        for f in range(4):
            for k in range(K):
                for t in range(2):
                    states[0][f, k, t, at, :] = ins[f][k, own, tiles[t]]
            strip[f, own, :] = strip_of([[ins[f][k, own, tiles[t]] for t in range(2)] for k in range(K)])
        for i in range(5):
            strip[4 + i, own, :] = strip_of([[ins[4 + i][own, tiles[t]].astype(jnp.float32) for t in range(2)]] * K)
        for t in range(2):
            sea = ins[5][own, tiles[t]] == 1
            rhos = []
            for k in range(K):
                wet[k, t, at, :] = jnp.where(sea & (ins[4][own, tiles[t]] > k), 1.0, 0.0)
                rhos.append(density(ins[T][k, own, tiles[t]], ins[S][k, own, tiles[t]], slope_of(k)))
            for k, value in enumerate(column_pressure(rhos)):
                states[0][PR, k, t, at, :] = value

    @pl.loop(0, rows // 8, unroll=6)
    def _(b):
        r = pl.multiple_of(8 * b + 8, 8)

        def write(i, k, t, value):
            coef[i, k, t, pl.ds(r, 8), :] = value

        tile_coefficients(
            lambda k, t, row: wet[k, t, pl.ds(row, 8), :],
            lambda i, t, row: ins[6 + i][pl.ds(pl.multiple_of(8 * b, 8), 8), tiles[t]],
            r,
            write,
        )

    for step in range(STEPS):
        @pl.loop(0, rows // 8, unroll=4)
        def _(b):
            r = pl.multiple_of(8 * b + 8, 8)

            def write(f, k, t, value):
                if step < STEPS - 1:
                    states[step + 1][f, k, t, pl.ds(r, 8), :] = value
                else:
                    outs[f][k, pl.ds(pl.multiple_of(8 * b, 8), 8), tiles[t]] = value

            advance_tiles(
                lambda f, k, t, row: states[step][f, k, t, pl.ds(row, 8), :],
                lambda i, k, t, row: coef[i, k, t, pl.ds(row, 8), :],
                r,
                write,
                last=step == STEPS - 1,
            )


def run_rims(*refs):
    geo_in, states, parts, strip_in = refs[0:5], refs[5:9], refs[9:13], refs[13]
    col_b, col_a, row_b, row_a = refs[14:18]
    outs = refs[18:22]
    north, cols, band, band_geo, band_wet, band_coef, sf, sg, sw, sc = refs[22:]
    rows = geo_in[0].shape[0]
    top = OFFSET + rows
    lon_even = lax.rem(lax.axis_index("lon"), 2) == 0
    lat = lax.axis_index("lat")
    lat_even = lax.rem(lat, 2) == 0
    lane = lane_index((8, LANES))
    tiles = [slice(t * LANES, (t + 1) * LANES) for t in range(2)]
    fold = lat == lax.axis_size("lat") - 1

    @pl.when(fold)
    def _():
        fold_rows(row_b, north)

    @pl.when(jnp.logical_not(fold))
    def _():
        north[...] = jnp.where(lat_even, row_a[...], row_b[...])

    def south_rows(p, lanes):
        rows_p = slice(4 * p, 4 * p + 4)
        return jnp.where(lat_even, row_b[rows_p, lanes], row_a[rows_p, lanes])

    def north_rows(p, lanes):
        return north[4 * p : 4 * p + 4, lanes]

    def place(dst, a, b):
        cols[0, dst, :] = jnp.where(lon_even, b, a)
        cols[1, dst, :] = jnp.where(lon_even, a, b)

    place(slice(OFFSET, top), col_a[...], col_b[...])
    place(slice(OFFSET - HALO, OFFSET), *(south_rows(PLANES, tiles[i]) for i in range(2)))
    place(slice(top, top + HALO), *(north_rows(PLANES, tiles[i]) for i in range(2)))

    own = ((16, 0), (8, rows - 16))
    far = ((24, 8), (8, rows - 16))
    halo = ((12, south_rows), (24, north_rows))
    blocks = ((8, 16), (16, 24))
    for side in range(2):
        put, first = own[side]
        place_h, rows_of = halo[side]
        for t in range(2):
            for f in range(4):
                for k in range(K):
                    band[side, 0, f, k, t, place_h : place_h + 4, :] = rows_of(3 * f + k, tiles[t])
            for i in range(5):
                band_geo[side, i, t, put : put + 16, :] = geo_in[i][first : first + 16, tiles[t]].astype(jnp.float32)
                band_geo[side, i, t, place_h : place_h + 4, :] = rows_of(12 + i, tiles[t])
            for k in range(K):
                for f in range(5):
                    band[side, 0, f, k, t, put : put + 16, :] = states[0][f, k, t, first + 8 : first + 24, :]
                    for step in range(1, STEPS):
                        at, start = far[side]
                        band[side, step, f, k, t, at : at + 8, :] = states[step][f, k, t, start + 8 : start + 16, :]
            at = 8 if side == 0 else 24
            rhos = [
                density(band[side, 0, T, k, t, at : at + 8, :], band[side, 0, S, k, t, at : at + 8, :], slope_of(k))
                for k in range(K)
            ]
            for k, value in enumerate(column_pressure(rhos)):
                band[side, 0, PR, k, t, at : at + 8, :] = value
            for at in (8, 16, 24):
                sea = band_geo[side, 1, t, at : at + 8, :] == 1.0
                for k in range(K):
                    wet = sea & (band_geo[side, 0, t, at : at + 8, :] > k)
                    band_wet[side, k, t, at : at + 8, :] = jnp.where(wet, 1.0, 0.0)

    own_rows = slice(OFFSET, top)
    for f in range(4):
        sf[0, f, own_rows, :] = strip_in[f]
    for i in range(5):
        sg[i, own_rows, :] = strip_in[4 + i]
    for side, (at, to) in enumerate(((8, OFFSET - 8), (24, top))):
        for f in range(4):
            sf[0, f, to : to + 8, :] = strip_of(
                [[band[side, 0, f, k, t, at : at + 8, :] for t in range(2)] for k in range(K)]
            )
        for i in range(5):
            sg[i, to : to + 8, :] = strip_of([[band_geo[side, i, t, at : at + 8, :] for t in range(2)]] * K)
    level = lane // 32
    slope = slope_of(level.astype(jnp.float32))

    def strip_pressure(t, s):
        rho = density(t, s, slope)
        one = jnp.where(lane >= 32, pltpu.roll(rho, 32, 1), 0.0)
        two = jnp.where(lane >= 64, pltpu.roll(rho, 64, 1), 0.0)
        return 0.5 * rho + (one + two)

    @pl.loop(0, (rows + 16) // 8, unroll=2)
    def _(b):
        r = pl.multiple_of(OFFSET - 8 + 8 * b, 8)
        at = pl.ds(r, 8)
        west, east = cols[0, at, :], cols[1, at, :]

        def insert(x, planes):
            for k, p in enumerate(planes):
                w = pltpu.roll(west, (32 * k - 4 * p) % LANES, 1)
                e = pltpu.roll(east, (32 * k + 28 - 4 * p) % LANES, 1)
                x = jnp.where((lane >= 32 * k) & (lane < 32 * k + 4), w, x)
                x = jnp.where((lane >= 32 * k + 28) & (lane < 32 * k + 32), e, x)
            return x

        for f in range(4):
            sf[0, f, at, :] = insert(sf[0, f, at, :], (3 * f, 3 * f + 1, 3 * f + 2))
        for i in range(5):
            sg[i, at, :] = insert(sg[i, at, :], (12 + i,) * K)
        sf[0, PR, at, :] = strip_pressure(sf[0, T, at, :], sf[0, S, at, :])
        wet = (sg[1, at, :] == 1.0) & (sg[0, at, :] > level.astype(jnp.float32))
        sw[at, :] = jnp.where(wet, 1.0, 0.0)

    def rolled(c):
        return pltpu.roll(c, LANES - 1, 1), pltpu.roll(c, 1, 1)

    @pl.loop(0, (rows + 16) // 8, unroll=7)
    def _(b):
        r = pl.multiple_of(OFFSET - 8 + 8 * b, 8)
        at = pl.ds(r, 8)
        c = sw[at, :]
        e, w = rolled(c)
        values = coefficients(
            c, e, w, sw[pl.ds(r + 1, 8), :], sw[pl.ds(r - 1, 8), :], sg[2, at, :], sg[3, at, :], sg[4, at, :]
        )
        for i, value in enumerate(values):
            sc[i, at, :] = value

    for side in range(2):
        @pl.loop(0, 2, unroll=2)
        def _(b):
            r = pl.multiple_of(blocks[side][0] + 8 * b, 8)

            def write(i, k, t, value):
                band_coef[side, i, k, t, pl.ds(r, 8), :] = value

            tile_coefficients(
                lambda k, t, row: band_wet[side, k, t, pl.ds(row, 8), :],
                lambda i, t, row: band_geo[side, 2 + i, t, pl.ds(row, 8), :],
                r,
                write,
            )

    for step in range(STEPS):
        final = step == STEPS - 1

        @pl.loop(0, 2 if final else 4, unroll=2)
        def _(n):
            side = n if final else lax.div(n, 2)
            r = pl.multiple_of(16 + 0 * n if final else 8 + 8 * (lax.rem(n, 2) + side), 8)

            def write(f, k, t, value):
                if final:
                    to = pl.multiple_of(side * (rows - 8), 8)
                    outs[f][k, pl.ds(to, 8), tiles[t]] = value
                else:
                    band[side, step + 1, f, k, t, pl.ds(r, 8), :] = value

            advance_tiles(
                lambda f, k, t, row: band[side, step, f, k, t, pl.ds(row, 8), :],
                lambda i, k, t, row: band_coef[side, i, k, t, pl.ds(row, 8), :],
                r,
                write,
                last=final,
            )

    def strip_step(step, r):
        at = pl.ds(r, 8)

        def around(f):
            c = sf[step % 2, f, at, :]
            return (c,) + rolled(c) + (sf[step % 2, f, pl.ds(r + 1, 8), :], sf[step % 2, f, pl.ds(r - 1, 8), :])

        return advance(around, lambda i: sc[i, at, :])

    for step in range(STEPS - 1):
        @pl.loop(0, (rows + 16) // 8, unroll=7)
        def _(b):
            r = pl.multiple_of(OFFSET - 8 + 8 * b, 8)
            new = strip_step(step, r)
            for f in range(4):
                sf[(step + 1) % 2, f, pl.ds(r, 8), :] = new[f]
            sf[(step + 1) % 2, PR, pl.ds(r, 8), :] = strip_pressure(new[T], new[S])

    def finish(q, source):
        new = strip_step(STEPS - 1, q + OFFSET)
        at = pl.ds(q, 8)
        for f in range(4):
            for k in range(K):
                low = pltpu.roll(new[f], (-32 * k - 4) % LANES, 1)
                high = pltpu.roll(new[f], 100 - 32 * k, 1)
                outs[f][k, at, tiles[0]] = jnp.where(lane < HALO, low, source[f][k, at, tiles[0]])
                outs[f][k, at, tiles[1]] = jnp.where(lane >= LANES - HALO, high, source[f][k, at, tiles[1]])

    finish(0, outs)
    finish(rows - 8, outs)

    @pl.loop(1, rows // 8 - 1, unroll=5)
    def _(b):
        finish(pl.multiple_of(8 * b, 8), parts)


def lon_pairs(nlon, nlat, partner):
    return [(i * nlat + j, partner(i) * nlat + j) for i in range(nlon) for j in range(nlat)]


def lat_pairs(nlon, nlat, odd):
    pairs = []
    for i in range(nlon):
        for j in range(nlat):
            up = (j % 2 == 0) != odd
            to, at = (j + 1 if up else j - 1), i
            if to < 0:
                continue
            if to == nlat:
                to, at = nlat - 1, nlon - 1 - i
            pairs.append((i * nlat + j, at * nlat + to))
    return pairs


def body(u_vel, v_vel, temp, salt, levels, land_sea, coriolis, inv_dx, inv_dy):
    args = (u_vel, v_vel, temp, salt, levels, land_sea, coriolis, inv_dx, inv_dy)
    rows, cols = levels.shape
    nlon, nlat = lax.axis_size("lon"), lax.axis_size("lat")
    axes = ("lon", "lat")
    params = pltpu.CompilerParams(vmem_limit_bytes=VMEM_LIMIT)
    f32 = jnp.float32
    column = jax.ShapeDtypeStruct((rows, LANES), f32)
    col_b, col_a = pl.pallas_call(
        pack_columns,
        in_specs=[pl.BlockSpec(memory_space=pltpu.HBM)] * 9,
        out_shape=(column, column),
        scratch_shapes=[pltpu.VMEM(a.shape, a.dtype) for a in args] + [pltpu.SemaphoreType.DMA((9,))],
        compiler_params=pltpu.CompilerParams(vmem_limit_bytes=62 * 1024 * 1024),
        name="pack_columns",
    )(*args)
    col_b = lax.ppermute(
        col_b, axes, lon_pairs(nlon, nlat, lambda i: (i + 1 if i % 2 else i - 1) % nlon)
    )
    col_a = lax.ppermute(col_a, axes, lon_pairs(nlon, nlat, lambda i: i ^ 1))

    def edge(block):
        def spec(a):
            if a.ndim == 3:
                return pl.BlockSpec((K, 8, cols), lambda i: (0, block, 0))
            return pl.BlockSpec((8, cols), lambda i: (block, 0))
        return [spec(a) for a in args]

    whole = pl.BlockSpec((rows, LANES), lambda i: (0, 0))
    row = jax.ShapeDtypeStruct((4 * PLANES + 4, cols), f32)
    row_spec = pl.BlockSpec(row.shape, lambda i: (0, 0))
    row_b, row_a = pl.pallas_call(
        pack_rows,
        grid=(1,),
        in_specs=edge(0) + edge(rows // 8 - 1) + [whole, whole],
        out_specs=(row_spec, row_spec),
        out_shape=(row, row),
        compiler_params=params,
        name="pack_rows",
    )(*args, *args, col_b, col_a)
    sent = row_a
    row_b = lax.ppermute(row_b, axes, lat_pairs(nlon, nlat, True))
    row_a = lax.ppermute(row_a, axes, lat_pairs(nlon, nlat, False))
    out = jax.ShapeDtypeStruct(u_vel.shape, f32)
    state = jax.ShapeDtypeStruct((5, K, 2, rows + 16, LANES), f32)
    vmem = pl.BlockSpec(memory_space=pltpu.VMEM)
    *kept, strip = pl.pallas_call(
        run_interior,
        in_specs=[vmem] * 9 + [pl.BlockSpec(memory_space=pl.ANY)],
        out_shape=(state,) * 4 + (out,) * 4 + (jax.ShapeDtypeStruct((9, rows, LANES), f32),),
        scratch_shapes=[
            pltpu.VMEM((11, K, 2, rows + 16, LANES), f32),
            pltpu.VMEM((K, 2, rows + 16, LANES), f32),
        ],
        compiler_params=params,
        cost_estimate=pl.CostEstimate(flops=30_000_000, bytes_accessed=16_000_000, transcendentals=0),
        name="run_interior",
    )(*args, sent)
    tall = rows + 32
    return pl.pallas_call(
        run_rims,
        out_shape=(out,) * 4,
        scratch_shapes=[
            pltpu.VMEM(row.shape, f32),
            pltpu.VMEM((2, tall, LANES), f32),
            pltpu.VMEM((2, 4, 5, K, 2, 40, LANES), f32),
            pltpu.VMEM((2, 5, 2, 40, LANES), f32),
            pltpu.VMEM((2, K, 2, 40, LANES), f32),
            pltpu.VMEM((2, 11, K, 2, 40, LANES), f32),
            pltpu.VMEM((2, 5, tall, LANES), f32),
            pltpu.VMEM((5, tall, LANES), f32),
            pltpu.VMEM((tall, LANES), f32),
            pltpu.VMEM((11, tall, LANES), f32),
        ],
        compiler_params=params,
        name="run_rims",
    )(*args[4:], *kept, strip, col_b, col_a, row_b, row_a)


def solution(mesh):
    block, plane = P(None, "lat", "lon"), P("lat", "lon")
    return jax.shard_map(
        body,
        mesh=mesh,
        in_specs=(block,) * 4 + (plane,) * 5,
        out_specs=(block,) * 4,
        check_vma=False,
    )
```

```python
import jax
import jax.numpy as jnp
from jax import lax
from jax.experimental import pallas as pl
from jax.experimental.pallas import tpu as pltpu
from jax.sharding import PartitionSpec as P

STEPS = 4
K = 3
HALO = 4
PLANES = 17
LANES = 128
OFFSET = 16
U, V, T, S, PR = range(5)
CXE, CXW, CYN, CYS, HXE, HXW, HYN, HYS, WET, WCEN, WCOR = range(11)
VMEM_LIMIT = 28 * 1024 * 1024


def plane_values(refs, p, rows, lanes):
    if p < 12:
        return refs[p // 3][p % 3, rows, lanes]
    return refs[4 + p - 12][rows, lanes].astype(jnp.float32)


def lane_index(shape):
    return lax.broadcasted_iota(jnp.int32, shape, len(shape) - 1)


def pack_columns(*refs):
    args, (out_b, out_a), ins, sems = refs[:9], refs[9:11], refs[11:20], refs[20]
    copies = [pltpu.make_async_copy(a, i, sems.at[n]) for n, (a, i) in enumerate(zip(args, ins))]
    for copy in copies:
        copy.start()
    rows, cols = ins[4].shape
    even = lax.rem(lax.axis_index("lon"), 2) == 0
    lane = lane_index((8, LANES))
    blocks = range(0, rows, 8)
    west, east = {}, {}
    for p in range(PLANES):
        if p % 3 == 0 or p > 12:
            copies[p // 3 if p < 12 else p - 8].wait()
        for r in blocks:
            w = plane_values(ins, p, slice(r, r + 8), slice(0, LANES))
            e = plane_values(ins, p, slice(r, r + 8), slice(cols - LANES, cols))
            w = pltpu.roll(w, 4 * p, 1) if p else w
            e = pltpu.roll(e, (4 * p + HALO) % LANES, 1)
            mine = lane >= 4 * p
            west[r] = jnp.where(mine, w, west[r]) if p else w
            east[r] = jnp.where(mine, e, east[r]) if p else e
    for r in blocks:
        out_a[r : r + 8, :] = jnp.where(even, east[r], west[r])
        out_b[r : r + 8, :] = jnp.where(even, west[r], east[r])


def pack_rows(*refs):
    south, north = refs[0:9], refs[9:18]
    col_b, col_a, _, out_b, out_a = refs[18:]
    rows = col_a.shape[0]
    even = lax.rem(lax.axis_index("lat"), 2) == 0
    for p in range(PLANES):
        s = plane_values(south, p, slice(0, 8), slice(None))[:HALO]
        n = plane_values(north, p, slice(0, 8), slice(None))[HALO:]
        out_a[4 * p : 4 * p + 4, :] = jnp.where(even, n, s)
        out_b[4 * p : 4 * p + 4, :] = jnp.where(even, s, n)
    for ref, lanes in ((col_a, slice(0, LANES)), (col_b, slice(LANES, 2 * LANES))):
        s = ref[0:HALO, :]
        n = ref[rows - HALO : rows, :]
        out_a[4 * PLANES : 4 * PLANES + 4, lanes] = jnp.where(even, n, s)
        out_b[4 * PLANES : 4 * PLANES + 4, lanes] = jnp.where(even, s, n)


def xor_rows(x, bit):
    row = lax.broadcasted_iota(jnp.int32, x.shape, 0)
    return jnp.where((row & bit) != 0, pltpu.roll(x, bit, 0), pltpu.roll(x, 8 - bit, 0))


def xor_lanes(x, bit):
    lane = lane_index(x.shape)
    if bit == LANES // 2:
        return pltpu.roll(x, bit, 1)
    return jnp.where((lane & bit) != 0, pltpu.roll(x, bit, 1), pltpu.roll(x, LANES - bit, 1))


def fold_rows(ref, out):
    lane = lane_index((8, LANES))
    row = lax.broadcasted_iota(jnp.int32, (8, LANES), 0)
    for r in range(0, 4 * PLANES + 4, 8):
        turned, short = [], []
        for t in range(2):
            x = ref[r : r + 8, t * LANES : (t + 1) * LANES]
            x = xor_rows(xor_rows(x, 1), 2)
            x = xor_lanes(xor_lanes(x, 1), 2)
            short.append(x)
            for bit in (4, 8, 16, 32, 64):
                x = xor_lanes(x, bit)
            turned.append(x)
        for t in range(2):
            x = turned[1 - t]
            if r < 24:
                x = -x
            if r + 8 > 4 * PLANES:
                packed = jnp.where(lane < 24, -short[t], short[t])
                x = jnp.where(row < 4, x, packed)
            out[r : r + 8, t * LANES : (t + 1) * LANES] = x


def density(t, s, slope):
    return t * (slope - 0.08 * t - 0.035 * s) + 0.7 * s


def slope_of(level):
    return -0.8 - 0.24 * ((level + 0.5) / K)


def column_pressure(rhos):
    above, out = None, []
    for rho in rhos:
        half = 0.5 * rho
        out.append(half if above is None else above + half)
        above = rho if above is None else above + rho
    return out


def coefficients(c, e, w, n, s, coriolis, idx, idy):
    hx, hy = 0.025 * idx, 0.025 * idy
    hxe, hxw, hyn, hys = c * e * hx, c * w * hx, c * n * hy, c * s * hy
    cx, cy = 1.2 * idx, 1.2 * idy
    cxe, cxw, cyn, cys = hxe * cx, hxw * cx, hyn * cy, hys * cy
    total = (cxe + cxw) + (cyn + cys)
    return cxe, cxw, cyn, cys, hxe, hxw, hyn, hys, c, c - 2.0 * total, 0.1 * c * coriolis


def advance(around, get):
    cxe, cxw, cyn, cys = get(CXE), get(CXW), get(CYN), get(CYS)
    hxe, hxw, hyn, hys = get(HXE), get(HXW), get(HYN), get(HYS)
    us, vs = around(U), around(V)
    u, v = us[0], vs[0]
    u2, v2 = u + u, v + v
    ae, aw = cxe - hxe * u2, cxw + hxw * u2
    an, as_ = cyn - hyn * v2, cys + hys * v2
    ac = get(WET) - ((ae + aw) + (an + as_))
    wcor = get(WCOR)
    p, pe, pw, pn, ps = around(PR)
    px = hxe * (pe - p) + hxw * (p - pw)
    py = hyn * (pn - p) + hys * (p - ps)

    def combine(xs, ac, ae, aw, an, as_):
        c, e, w, n, s = xs
        return (ac * c + (ae * e + aw * w)) + (an * n + as_ * s)

    u_new = combine(us, ac, ae, aw, an, as_) + (wcor * v - px)
    v_new = combine(vs, ac, ae, aw, an, as_) - (wcor * u + py)
    ae = cxe - hxe * (u + us[1])
    aw = cxw + hxw * (u + us[2])
    an = cyn - hyn * (v + vs[3])
    as_ = cys + hys * (v + vs[4])
    ac = get(WCEN) + ((ae + aw) + (an + as_))
    t_new = combine(around(T), ac, ae, aw, an, as_)
    s_new = combine(around(S), ac, ae, aw, an, as_)
    return u_new, v_new, t_new, s_new


def east_west(c, other, t):
    lane = lane_index(c.shape)
    if t == 0:
        e = pltpu.roll(jnp.where(lane == 0, other, c), LANES - 1, 1)
        w = pltpu.roll(c, 1, 1)
    else:
        e = pltpu.roll(c, LANES - 1, 1)
        w = pltpu.roll(jnp.where(lane == LANES - 1, other, c), 1, 1)
    return e, w


def advance_tiles(field, coef, r, write, last=False):
    for t in range(2):
        above = None
        for k in range(K):
            def around(f):
                c = field(f, k, t, r)
                e, w = east_west(c, field(f, k, 1 - t, r), t)
                return c, e, w, field(f, k, t, r + 1), field(f, k, t, r - 1)

            new = advance(around, lambda i: coef(i, k, t, r))
            for f in range(4):
                write(f, k, t, new[f])
            if not last:
                rho = density(new[T], new[S], slope_of(k))
                half = 0.5 * rho
                write(PR, k, t, half if k == 0 else above + half)
                above = rho if k == 0 else above + rho


def tile_coefficients(wet, geo, r, write):
    for k in range(K):
        for t in range(2):
            c = wet(k, t, r)
            e, w = east_west(c, wet(k, 1 - t, r), t)
            values = coefficients(
                c, e, w, wet(k, t, r + 1), wet(k, t, r - 1), geo(0, t, r), geo(1, t, r), geo(2, t, r)
            )
            for i, value in enumerate(values):
                write(i, k, t, value)


def strip_of(tiles):
    lane = lane_index((8, LANES))
    out = None
    for k, (low, high) in enumerate(tiles):
        x = pltpu.roll(low, 32 * k + 4, 1)
        y = pltpu.roll(high, (32 * k - 100) % LANES, 1)
        both = jnp.where(lane >= 32 * k + 16, y, x)
        out = both if k == 0 else jnp.where(lane >= 32 * k, both, out)
    return out


def prepare_interior(*refs):
    ins, (state, coef, strip, wet) = refs[:9], refs[10:]
    rows = ins[4].shape[0]
    tiles = [slice(t * LANES, (t + 1) * LANES) for t in range(2)]

    @pl.loop(0, rows // 8, unroll=6)
    def _(b):
        q = pl.multiple_of(8 * b, 8)
        r = pl.multiple_of(8 * b + 8, 8)
        at, own = pl.ds(r, 8), pl.ds(q, 8)
        for f in range(4):
            for k in range(K):
                for t in range(2):
                    state[f, k, t, at, :] = ins[f][k, own, tiles[t]]
            strip[f, own, :] = strip_of([[ins[f][k, own, tiles[t]] for t in range(2)] for k in range(K)])
        for i in range(5):
            strip[4 + i, own, :] = strip_of([[ins[4 + i][own, tiles[t]].astype(jnp.float32) for t in range(2)]] * K)
        for t in range(2):
            sea = ins[5][own, tiles[t]] == 1
            rhos = []
            for k in range(K):
                wet[k, t, at, :] = jnp.where(sea & (ins[4][own, tiles[t]] > k), 1.0, 0.0)
                rhos.append(density(ins[T][k, own, tiles[t]], ins[S][k, own, tiles[t]], slope_of(k)))
            for k, value in enumerate(column_pressure(rhos)):
                state[PR, k, t, at, :] = value

    @pl.loop(0, rows // 8, unroll=6)
    def _(b):
        r = pl.multiple_of(8 * b + 8, 8)

        def write(i, k, t, value):
            coef[i, k, t, pl.ds(r, 8), :] = value

        tile_coefficients(
            lambda k, t, row: wet[k, t, pl.ds(row, 8), :],
            lambda i, t, row: ins[6 + i][pl.ds(pl.multiple_of(8 * b, 8), 8), tiles[t]],
            r,
            write,
        )


def run_interior(*refs):
    coef, states, outs = refs[1], (refs[0],) + refs[3:6], refs[6:10]
    rows = outs[0].shape[1]
    tiles = [slice(t * LANES, (t + 1) * LANES) for t in range(2)]

    for step in range(STEPS):
        @pl.loop(0, rows // 8, unroll=6)
        def _(b):
            r = pl.multiple_of(8 * b + 8, 8)

            def write(f, k, t, value):
                if step < STEPS - 1:
                    states[step + 1][f, k, t, pl.ds(r, 8), :] = value
                else:
                    outs[f][k, pl.ds(pl.multiple_of(8 * b, 8), 8), tiles[t]] = value

            advance_tiles(
                lambda f, k, t, row: states[step][f, k, t, pl.ds(row, 8), :],
                lambda i, k, t, row: coef[i, k, t, pl.ds(row, 8), :],
                r,
                write,
                last=step == STEPS - 1,
            )


def run_rims(*refs):
    geo_in, states, parts, strip_in = refs[0:5], refs[5:9], refs[9:13], refs[13]
    col_b, col_a, row_b, row_a = refs[14:18]
    outs = refs[18:22]
    north, cols, band, band_geo, band_wet, band_coef, sf, sg, sw, sc = refs[22:]
    rows = geo_in[0].shape[0]
    top = OFFSET + rows
    lon_even = lax.rem(lax.axis_index("lon"), 2) == 0
    lat = lax.axis_index("lat")
    lat_even = lax.rem(lat, 2) == 0
    lane = lane_index((8, LANES))
    tiles = [slice(t * LANES, (t + 1) * LANES) for t in range(2)]
    fold = lat == lax.axis_size("lat") - 1

    @pl.when(fold)
    def _():
        fold_rows(row_b, north)

    @pl.when(jnp.logical_not(fold))
    def _():
        north[...] = jnp.where(lat_even, row_a[...], row_b[...])

    def south_rows(p, lanes):
        rows_p = slice(4 * p, 4 * p + 4)
        return jnp.where(lat_even, row_b[rows_p, lanes], row_a[rows_p, lanes])

    def north_rows(p, lanes):
        return north[4 * p : 4 * p + 4, lanes]

    def place(dst, a, b):
        cols[0, dst, :] = jnp.where(lon_even, b, a)
        cols[1, dst, :] = jnp.where(lon_even, a, b)

    place(slice(OFFSET, top), col_a[...], col_b[...])
    place(slice(OFFSET - HALO, OFFSET), *(south_rows(PLANES, tiles[i]) for i in range(2)))
    place(slice(top, top + HALO), *(north_rows(PLANES, tiles[i]) for i in range(2)))

    own = ((16, 0), (8, rows - 16))
    far = ((24, 8), (8, rows - 16))
    halo = ((12, south_rows), (24, north_rows))
    blocks = ((8, 16), (16, 24))
    for side in range(2):
        put, first = own[side]
        place_h, rows_of = halo[side]
        for t in range(2):
            for f in range(4):
                for k in range(K):
                    band[side, 0, f, k, t, place_h : place_h + 4, :] = rows_of(3 * f + k, tiles[t])
            for i in range(5):
                band_geo[side, i, t, put : put + 16, :] = geo_in[i][first : first + 16, tiles[t]].astype(jnp.float32)
                band_geo[side, i, t, place_h : place_h + 4, :] = rows_of(12 + i, tiles[t])
            for k in range(K):
                for f in range(5):
                    band[side, 0, f, k, t, put : put + 16, :] = states[0][f, k, t, first + 8 : first + 24, :]
                    for step in range(1, STEPS):
                        at, start = far[side]
                        band[side, step, f, k, t, at : at + 8, :] = states[step][f, k, t, start + 8 : start + 16, :]
            at = 8 if side == 0 else 24
            rhos = [
                density(band[side, 0, T, k, t, at : at + 8, :], band[side, 0, S, k, t, at : at + 8, :], slope_of(k))
                for k in range(K)
            ]
            for k, value in enumerate(column_pressure(rhos)):
                band[side, 0, PR, k, t, at : at + 8, :] = value
            for at in (8, 16, 24):
                sea = band_geo[side, 1, t, at : at + 8, :] == 1.0
                for k in range(K):
                    wet = sea & (band_geo[side, 0, t, at : at + 8, :] > k)
                    band_wet[side, k, t, at : at + 8, :] = jnp.where(wet, 1.0, 0.0)

    own_rows = slice(OFFSET, top)
    for f in range(4):
        sf[0, f, own_rows, :] = strip_in[f]
    for i in range(5):
        sg[i, own_rows, :] = strip_in[4 + i]
    for side, (at, to) in enumerate(((8, OFFSET - 8), (24, top))):
        for f in range(4):
            sf[0, f, to : to + 8, :] = strip_of(
                [[band[side, 0, f, k, t, at : at + 8, :] for t in range(2)] for k in range(K)]
            )
        for i in range(5):
            sg[i, to : to + 8, :] = strip_of([[band_geo[side, i, t, at : at + 8, :] for t in range(2)]] * K)
    level = lane // 32
    slope = slope_of(level.astype(jnp.float32))

    def strip_pressure(t, s):
        rho = density(t, s, slope)
        one = jnp.where(lane >= 32, pltpu.roll(rho, 32, 1), 0.0)
        two = jnp.where(lane >= 64, pltpu.roll(rho, 64, 1), 0.0)
        return 0.5 * rho + (one + two)

    @pl.loop(0, (rows + 16) // 8, unroll=2)
    def _(b):
        r = pl.multiple_of(OFFSET - 8 + 8 * b, 8)
        at = pl.ds(r, 8)
        west, east = cols[0, at, :], cols[1, at, :]

        def insert(x, planes):
            for k, p in enumerate(planes):
                w = pltpu.roll(west, (32 * k - 4 * p) % LANES, 1)
                e = pltpu.roll(east, (32 * k + 28 - 4 * p) % LANES, 1)
                x = jnp.where((lane >= 32 * k) & (lane < 32 * k + 4), w, x)
                x = jnp.where((lane >= 32 * k + 28) & (lane < 32 * k + 32), e, x)
            return x

        for f in range(4):
            sf[0, f, at, :] = insert(sf[0, f, at, :], (3 * f, 3 * f + 1, 3 * f + 2))
        for i in range(5):
            sg[i, at, :] = insert(sg[i, at, :], (12 + i,) * K)
        sf[0, PR, at, :] = strip_pressure(sf[0, T, at, :], sf[0, S, at, :])
        wet = (sg[1, at, :] == 1.0) & (sg[0, at, :] > level.astype(jnp.float32))
        sw[at, :] = jnp.where(wet, 1.0, 0.0)

    def rolled(c):
        return pltpu.roll(c, LANES - 1, 1), pltpu.roll(c, 1, 1)

    @pl.loop(0, (rows + 16) // 8, unroll=7)
    def _(b):
        r = pl.multiple_of(OFFSET - 8 + 8 * b, 8)
        at = pl.ds(r, 8)
        c = sw[at, :]
        e, w = rolled(c)
        values = coefficients(
            c, e, w, sw[pl.ds(r + 1, 8), :], sw[pl.ds(r - 1, 8), :], sg[2, at, :], sg[3, at, :], sg[4, at, :]
        )
        for i, value in enumerate(values):
            sc[i, at, :] = value

    for side in range(2):
        @pl.loop(0, 2, unroll=2)
        def _(b):
            r = pl.multiple_of(blocks[side][0] + 8 * b, 8)

            def write(i, k, t, value):
                band_coef[side, i, k, t, pl.ds(r, 8), :] = value

            tile_coefficients(
                lambda k, t, row: band_wet[side, k, t, pl.ds(row, 8), :],
                lambda i, t, row: band_geo[side, 2 + i, t, pl.ds(row, 8), :],
                r,
                write,
            )

    for step in range(STEPS):
        final = step == STEPS - 1

        @pl.loop(0, 2 if final else 4, unroll=2)
        def _(n):
            side = n if final else lax.div(n, 2)
            r = pl.multiple_of(16 + 0 * n if final else 8 + 8 * (lax.rem(n, 2) + side), 8)

            def write(f, k, t, value):
                if final:
                    to = pl.multiple_of(side * (rows - 8), 8)
                    outs[f][k, pl.ds(to, 8), tiles[t]] = value
                else:
                    band[side, step + 1, f, k, t, pl.ds(r, 8), :] = value

            advance_tiles(
                lambda f, k, t, row: band[side, step, f, k, t, pl.ds(row, 8), :],
                lambda i, k, t, row: band_coef[side, i, k, t, pl.ds(row, 8), :],
                r,
                write,
                last=final,
            )

    def strip_step(step, r):
        at = pl.ds(r, 8)

        def around(f):
            c = sf[step % 2, f, at, :]
            return (c,) + rolled(c) + (sf[step % 2, f, pl.ds(r + 1, 8), :], sf[step % 2, f, pl.ds(r - 1, 8), :])

        return advance(around, lambda i: sc[i, at, :])

    for step in range(STEPS - 1):
        @pl.loop(0, (rows + 16) // 8, unroll=7)
        def _(b):
            r = pl.multiple_of(OFFSET - 8 + 8 * b, 8)
            new = strip_step(step, r)
            for f in range(4):
                sf[(step + 1) % 2, f, pl.ds(r, 8), :] = new[f]
            sf[(step + 1) % 2, PR, pl.ds(r, 8), :] = strip_pressure(new[T], new[S])

    def finish(q, source):
        new = strip_step(STEPS - 1, q + OFFSET)
        at = pl.ds(q, 8)
        for f in range(4):
            for k in range(K):
                low = pltpu.roll(new[f], (-32 * k - 4) % LANES, 1)
                high = pltpu.roll(new[f], 100 - 32 * k, 1)
                outs[f][k, at, tiles[0]] = jnp.where(lane < HALO, low, source[f][k, at, tiles[0]])
                outs[f][k, at, tiles[1]] = jnp.where(lane >= LANES - HALO, high, source[f][k, at, tiles[1]])

    finish(0, outs)
    finish(rows - 8, outs)

    @pl.loop(1, rows // 8 - 1, unroll=5)
    def _(b):
        finish(pl.multiple_of(8 * b, 8), parts)


def lon_pairs(nlon, nlat, partner):
    return [(i * nlat + j, partner(i) * nlat + j) for i in range(nlon) for j in range(nlat)]


def lat_pairs(nlon, nlat, odd):
    pairs = []
    for i in range(nlon):
        for j in range(nlat):
            up = (j % 2 == 0) != odd
            to, at = (j + 1 if up else j - 1), i
            if to < 0:
                continue
            if to == nlat:
                to, at = nlat - 1, nlon - 1 - i
            pairs.append((i * nlat + j, at * nlat + to))
    return pairs


def body(u_vel, v_vel, temp, salt, levels, land_sea, coriolis, inv_dx, inv_dy):
    args = (u_vel, v_vel, temp, salt, levels, land_sea, coriolis, inv_dx, inv_dy)
    rows, cols = levels.shape
    nlon, nlat = lax.axis_size("lon"), lax.axis_size("lat")
    axes = ("lon", "lat")
    params = pltpu.CompilerParams(vmem_limit_bytes=VMEM_LIMIT)
    f32 = jnp.float32
    column = jax.ShapeDtypeStruct((rows, LANES), f32)
    col_b, col_a = pl.pallas_call(
        pack_columns,
        in_specs=[pl.BlockSpec(memory_space=pltpu.HBM)] * 9,
        out_shape=(column, column),
        scratch_shapes=[pltpu.VMEM(a.shape, a.dtype) for a in args] + [pltpu.SemaphoreType.DMA((9,))],
        compiler_params=pltpu.CompilerParams(vmem_limit_bytes=62 * 1024 * 1024),
        name="pack_columns",
    )(*args)
    packed = col_b
    col_b = lax.ppermute(
        col_b, axes, lon_pairs(nlon, nlat, lambda i: (i + 1 if i % 2 else i - 1) % nlon)
    )
    col_a = lax.ppermute(col_a, axes, lon_pairs(nlon, nlat, lambda i: i ^ 1))

    state = jax.ShapeDtypeStruct((5, K, 2, rows + 16, LANES), f32)
    vmem = pl.BlockSpec(memory_space=pltpu.VMEM)
    state0, coef, strip = pl.pallas_call(
        prepare_interior,
        in_specs=[vmem] * 9 + [pl.BlockSpec(memory_space=pl.ANY)],
        out_shape=(
            state,
            jax.ShapeDtypeStruct((11, K, 2, rows + 16, LANES), f32),
            jax.ShapeDtypeStruct((9, rows, LANES), f32),
        ),
        scratch_shapes=[pltpu.VMEM((K, 2, rows + 16, LANES), f32)],
        compiler_params=params,
        cost_estimate=pl.CostEstimate(flops=10_000_000, bytes_accessed=8_000_000, transcendentals=0),
        name="prepare_interior",
    )(*args, packed)

    def edge(block):
        def spec(a):
            if a.ndim == 3:
                return pl.BlockSpec((K, 8, cols), lambda i: (0, block, 0))
            return pl.BlockSpec((8, cols), lambda i: (block, 0))
        return [spec(a) for a in args]

    whole = pl.BlockSpec((rows, LANES), lambda i: (0, 0))
    row = jax.ShapeDtypeStruct((4 * PLANES + 4, cols), f32)
    row_spec = pl.BlockSpec(row.shape, lambda i: (0, 0))
    row_b, row_a = pl.pallas_call(
        pack_rows,
        grid=(1,),
        in_specs=edge(0) + edge(rows // 8 - 1) + [whole, whole, pl.BlockSpec(memory_space=pl.ANY)],
        out_specs=(row_spec, row_spec),
        out_shape=(row, row),
        compiler_params=params,
        name="pack_rows",
    )(*args, *args, col_b, col_a, strip)
    sent = row_b
    row_b = lax.ppermute(row_b, axes, lat_pairs(nlon, nlat, True))
    row_a = lax.ppermute(row_a, axes, lat_pairs(nlon, nlat, False))
    out = jax.ShapeDtypeStruct(u_vel.shape, f32)
    *kept, = pl.pallas_call(
        run_interior,
        in_specs=[vmem] * 2 + [pl.BlockSpec(memory_space=pl.ANY)],
        out_shape=(state,) * 3 + (out,) * 4,
        compiler_params=params,
        cost_estimate=pl.CostEstimate(flops=30_000_000, bytes_accessed=16_000_000, transcendentals=0),
        name="run_interior",
    )(state0, coef, sent)
    tall = rows + 32
    return pl.pallas_call(
        run_rims,
        out_shape=(out,) * 4,
        scratch_shapes=[
            pltpu.VMEM(row.shape, f32),
            pltpu.VMEM((2, tall, LANES), f32),
            pltpu.VMEM((2, 4, 5, K, 2, 40, LANES), f32),
            pltpu.VMEM((2, 5, 2, 40, LANES), f32),
            pltpu.VMEM((2, K, 2, 40, LANES), f32),
            pltpu.VMEM((2, 11, K, 2, 40, LANES), f32),
            pltpu.VMEM((2, 5, tall, LANES), f32),
            pltpu.VMEM((5, tall, LANES), f32),
            pltpu.VMEM((tall, LANES), f32),
            pltpu.VMEM((11, tall, LANES), f32),
        ],
        compiler_params=params,
        name="run_rims",
    )(*args[4:], state0, *kept, strip, col_b, col_a, row_b, row_a)


def solution(mesh):
    block, plane = P(None, "lat", "lon"), P("lat", "lon")
    return jax.shard_map(
        body,
        mesh=mesh,
        in_specs=(block,) * 4 + (plane,) * 5,
        out_specs=(block,) * 4,
        check_vma=False,
    )
```

```python
import jax
import jax.numpy as jnp
from jax import lax
from jax.experimental import pallas as pl
from jax.experimental.pallas import tpu as pltpu
from jax.sharding import PartitionSpec as P

STEPS = 4
K = 3
HALO = 4
PLANES = 17
LANES = 128
OFFSET = 16
U, V, T, S, PR = range(5)
CXE, CXW, CYN, CYS, HXE, HXW, HYN, HYS, WET, WCEN, WCOR = range(11)
VMEM_LIMIT = 28 * 1024 * 1024


def plane_values(refs, p, rows, lanes):
    if p < 12:
        return refs[p // 3][p % 3, rows, lanes]
    return refs[4 + p - 12][rows, lanes].astype(jnp.float32)


def lane_index(shape):
    return lax.broadcasted_iota(jnp.int32, shape, len(shape) - 1)


def pack_columns(*refs):
    args, (out_b, out_a), ins, sems = refs[:9], refs[9:11], refs[11:20], refs[20]
    copies = [pltpu.make_async_copy(a, i, sems.at[n]) for n, (a, i) in enumerate(zip(args, ins))]
    for copy in copies:
        copy.start()
    rows, cols = ins[4].shape
    even = lax.rem(lax.axis_index("lon"), 2) == 0
    lane = lane_index((8, LANES))
    blocks = range(0, rows, 8)
    west, east = {}, {}
    for p in range(PLANES):
        if p % 3 == 0 or p > 12:
            copies[p // 3 if p < 12 else p - 8].wait()
        for r in blocks:
            w = plane_values(ins, p, slice(r, r + 8), slice(0, LANES))
            e = plane_values(ins, p, slice(r, r + 8), slice(cols - LANES, cols))
            x = pltpu.roll(jnp.where(lane < LANES // 2, w, e), 4 * p + HALO, 1)
            west[r] = jnp.where(lane >= 4 * p + HALO, x, west[r]) if p else x
            east[r] = jnp.where(lane >= 4 * p, x, east[r]) if p else x
    for r in blocks:
        west[r] = pltpu.roll(west[r], LANES - HALO, 1)
    for r in blocks:
        out_a[r : r + 8, :] = jnp.where(even, east[r], west[r])
        out_b[r : r + 8, :] = jnp.where(even, west[r], east[r])


def pack_rows(*refs):
    south, north = refs[0:9], refs[9:18]
    col_b, col_a, _, out_b, out_a = refs[18:]
    rows = col_a.shape[0]
    even = lax.rem(lax.axis_index("lat"), 2) == 0
    for p in range(PLANES):
        s = plane_values(south, p, slice(0, 8), slice(None))[:HALO]
        n = plane_values(north, p, slice(0, 8), slice(None))[HALO:]
        out_a[4 * p : 4 * p + 4, :] = jnp.where(even, n, s)
        out_b[4 * p : 4 * p + 4, :] = jnp.where(even, s, n)
    for ref, lanes in ((col_a, slice(0, LANES)), (col_b, slice(LANES, 2 * LANES))):
        s = ref[0:HALO, :]
        n = ref[rows - HALO : rows, :]
        out_a[4 * PLANES : 4 * PLANES + 4, lanes] = jnp.where(even, n, s)
        out_b[4 * PLANES : 4 * PLANES + 4, lanes] = jnp.where(even, s, n)


def xor_rows(x, bit):
    row = lax.broadcasted_iota(jnp.int32, x.shape, 0)
    return jnp.where((row & bit) != 0, pltpu.roll(x, bit, 0), pltpu.roll(x, 8 - bit, 0))


def xor_lanes(x, bit):
    lane = lane_index(x.shape)
    if bit == LANES // 2:
        return pltpu.roll(x, bit, 1)
    return jnp.where((lane & bit) != 0, pltpu.roll(x, bit, 1), pltpu.roll(x, LANES - bit, 1))


def fold_rows(ref, out):
    lane = lane_index((8, LANES))
    row = lax.broadcasted_iota(jnp.int32, (8, LANES), 0)
    for r in range(0, 4 * PLANES + 4, 8):
        turned, short = [], []
        for t in range(2):
            x = ref[r : r + 8, t * LANES : (t + 1) * LANES]
            x = xor_rows(xor_rows(x, 1), 2)
            x = xor_lanes(xor_lanes(x, 1), 2)
            short.append(x)
            for bit in (4, 8, 16, 32, 64):
                x = xor_lanes(x, bit)
            turned.append(x)
        for t in range(2):
            x = turned[1 - t]
            if r < 24:
                x = -x
            if r + 8 > 4 * PLANES:
                packed = jnp.where(lane < 24, -short[t], short[t])
                x = jnp.where(row < 4, x, packed)
            out[r : r + 8, t * LANES : (t + 1) * LANES] = x


def density(t, s, slope):
    return t * (slope - 0.08 * t - 0.035 * s) + 0.7 * s


def slope_of(level):
    return -0.8 - 0.24 * ((level + 0.5) / K)


def column_pressure(rhos):
    above, out = None, []
    for rho in rhos:
        half = 0.5 * rho
        out.append(half if above is None else above + half)
        above = rho if above is None else above + rho
    return out


def coefficients(c, e, w, n, s, coriolis, idx, idy):
    hx, hy = 0.025 * idx, 0.025 * idy
    hxe, hxw, hyn, hys = c * e * hx, c * w * hx, c * n * hy, c * s * hy
    cx, cy = 1.2 * idx, 1.2 * idy
    cxe, cxw, cyn, cys = hxe * cx, hxw * cx, hyn * cy, hys * cy
    total = (cxe + cxw) + (cyn + cys)
    return cxe, cxw, cyn, cys, hxe, hxw, hyn, hys, c, c - 2.0 * total, 0.1 * c * coriolis


def advance(around, get):
    cxe, cxw, cyn, cys = get(CXE), get(CXW), get(CYN), get(CYS)
    hxe, hxw, hyn, hys = get(HXE), get(HXW), get(HYN), get(HYS)
    us, vs = around(U), around(V)
    u, v = us[0], vs[0]
    u2, v2 = u + u, v + v
    ae, aw = cxe - hxe * u2, cxw + hxw * u2
    an, as_ = cyn - hyn * v2, cys + hys * v2
    ac = get(WET) - ((ae + aw) + (an + as_))
    wcor = get(WCOR)
    p, pe, pw, pn, ps = around(PR)
    px = hxe * (pe - p) + hxw * (p - pw)
    py = hyn * (pn - p) + hys * (p - ps)

    def combine(xs, ac, ae, aw, an, as_):
        c, e, w, n, s = xs
        return (ac * c + (ae * e + aw * w)) + (an * n + as_ * s)

    u_new = combine(us, ac, ae, aw, an, as_) + (wcor * v - px)
    v_new = combine(vs, ac, ae, aw, an, as_) - (wcor * u + py)
    ae = cxe - hxe * (u + us[1])
    aw = cxw + hxw * (u + us[2])
    an = cyn - hyn * (v + vs[3])
    as_ = cys + hys * (v + vs[4])
    ac = get(WCEN) + ((ae + aw) + (an + as_))
    t_new = combine(around(T), ac, ae, aw, an, as_)
    s_new = combine(around(S), ac, ae, aw, an, as_)
    return u_new, v_new, t_new, s_new


def east_west(c, other, t):
    lane = lane_index(c.shape)
    if t == 0:
        e = pltpu.roll(jnp.where(lane == 0, other, c), LANES - 1, 1)
        w = pltpu.roll(c, 1, 1)
    else:
        e = pltpu.roll(c, LANES - 1, 1)
        w = pltpu.roll(jnp.where(lane == LANES - 1, other, c), 1, 1)
    return e, w


def advance_tiles(field, coef, r, write, last=False):
    for t in range(2):
        above = None
        for k in range(K):
            def around(f):
                c = field(f, k, t, r)
                e, w = east_west(c, field(f, k, 1 - t, r), t)
                return c, e, w, field(f, k, t, r + 1), field(f, k, t, r - 1)

            new = advance(around, lambda i: coef(i, k, t, r))
            for f in range(4):
                write(f, k, t, new[f])
            if not last:
                rho = density(new[T], new[S], slope_of(k))
                half = 0.5 * rho
                write(PR, k, t, half if k == 0 else above + half)
                above = rho if k == 0 else above + rho


def tile_coefficients(wet, geo, r, write):
    for k in range(K):
        for t in range(2):
            c = wet(k, t, r)
            e, w = east_west(c, wet(k, 1 - t, r), t)
            values = coefficients(
                c, e, w, wet(k, t, r + 1), wet(k, t, r - 1), geo(0, t, r), geo(1, t, r), geo(2, t, r)
            )
            for i, value in enumerate(values):
                write(i, k, t, value)


def strip_of(tiles):
    lane = lane_index((8, LANES))
    out = None
    for k, (low, high) in enumerate(tiles):
        x = pltpu.roll(low, 32 * k + 4, 1)
        y = pltpu.roll(high, (32 * k - 100) % LANES, 1)
        both = jnp.where(lane >= 32 * k + 16, y, x)
        out = both if k == 0 else jnp.where(lane >= 32 * k, both, out)
    return out


def prepare_interior(*refs):
    ins, (state, coef, strip, wet) = refs[:9], refs[9:]
    rows = ins[4].shape[0]
    tiles = [slice(t * LANES, (t + 1) * LANES) for t in range(2)]

    @pl.loop(0, rows // 8, unroll=6)
    def _(b):
        q = pl.multiple_of(8 * b, 8)
        r = pl.multiple_of(8 * b + 8, 8)
        at, own = pl.ds(r, 8), pl.ds(q, 8)
        for f in range(4):
            for k in range(K):
                for t in range(2):
                    state[f, k, t, at, :] = ins[f][k, own, tiles[t]]
            strip[f, own, :] = strip_of([[ins[f][k, own, tiles[t]] for t in range(2)] for k in range(K)])
        for i in range(5):
            strip[4 + i, own, :] = strip_of([[ins[4 + i][own, tiles[t]].astype(jnp.float32) for t in range(2)]] * K)
        for t in range(2):
            sea = ins[5][own, tiles[t]] == 1
            rhos = []
            for k in range(K):
                wet[k, t, at, :] = jnp.where(sea & (ins[4][own, tiles[t]] > k), 1.0, 0.0)
                rhos.append(density(ins[T][k, own, tiles[t]], ins[S][k, own, tiles[t]], slope_of(k)))
            for k, value in enumerate(column_pressure(rhos)):
                state[PR, k, t, at, :] = value

    @pl.loop(0, rows // 8, unroll=6)
    def _(b):
        r = pl.multiple_of(8 * b + 8, 8)

        def write(i, k, t, value):
            coef[i, k, t, pl.ds(r, 8), :] = value

        tile_coefficients(
            lambda k, t, row: wet[k, t, pl.ds(row, 8), :],
            lambda i, t, row: ins[6 + i][pl.ds(pl.multiple_of(8 * b, 8), 8), tiles[t]],
            r,
            write,
        )


def run_interior(*refs):
    coef, states, outs = refs[1], (refs[0],) + refs[3:6], refs[6:10]
    rows = outs[0].shape[1]
    tiles = [slice(t * LANES, (t + 1) * LANES) for t in range(2)]

    for step in range(STEPS):
        @pl.loop(0, rows // 8, unroll=6)
        def _(b):
            r = pl.multiple_of(8 * b + 8, 8)

            def write(f, k, t, value):
                if step < STEPS - 1:
                    states[step + 1][f, k, t, pl.ds(r, 8), :] = value
                else:
                    outs[f][k, pl.ds(pl.multiple_of(8 * b, 8), 8), tiles[t]] = value

            advance_tiles(
                lambda f, k, t, row: states[step][f, k, t, pl.ds(row, 8), :],
                lambda i, k, t, row: coef[i, k, t, pl.ds(row, 8), :],
                r,
                write,
                last=step == STEPS - 1,
            )


def run_rims(*refs):
    geo_in, states, parts, strip_in = refs[0:5], refs[5:9], refs[9:13], refs[13]
    col_b, col_a, row_b, row_a = refs[14:18]
    outs = refs[18:22]
    north, cols, band, band_geo, band_wet, band_coef, sf, sg, sw, sc = refs[22:]
    rows = geo_in[0].shape[0]
    top = OFFSET + rows
    lon_even = lax.rem(lax.axis_index("lon"), 2) == 0
    lat = lax.axis_index("lat")
    lat_even = lax.rem(lat, 2) == 0
    lane = lane_index((8, LANES))
    tiles = [slice(t * LANES, (t + 1) * LANES) for t in range(2)]
    fold = lat == lax.axis_size("lat") - 1

    @pl.when(fold)
    def _():
        fold_rows(row_b, north)

    @pl.when(jnp.logical_not(fold))
    def _():
        north[...] = jnp.where(lat_even, row_a[...], row_b[...])

    def south_rows(p, lanes):
        rows_p = slice(4 * p, 4 * p + 4)
        return jnp.where(lat_even, row_b[rows_p, lanes], row_a[rows_p, lanes])

    def north_rows(p, lanes):
        return north[4 * p : 4 * p + 4, lanes]

    def place(dst, a, b):
        cols[0, dst, :] = jnp.where(lon_even, b, a)
        cols[1, dst, :] = jnp.where(lon_even, a, b)

    place(slice(OFFSET, top), col_a[...], col_b[...])
    place(slice(OFFSET - HALO, OFFSET), *(south_rows(PLANES, tiles[i]) for i in range(2)))
    place(slice(top, top + HALO), *(north_rows(PLANES, tiles[i]) for i in range(2)))

    own = ((16, 0), (8, rows - 16))
    far = ((24, 8), (8, rows - 16))
    halo = ((12, south_rows), (24, north_rows))
    blocks = ((8, 16), (16, 24))
    for side in range(2):
        put, first = own[side]
        place_h, rows_of = halo[side]
        for t in range(2):
            for f in range(4):
                for k in range(K):
                    band[side, 0, f, k, t, place_h : place_h + 4, :] = rows_of(3 * f + k, tiles[t])
            for i in range(5):
                band_geo[side, i, t, put : put + 16, :] = geo_in[i][first : first + 16, tiles[t]].astype(jnp.float32)
                band_geo[side, i, t, place_h : place_h + 4, :] = rows_of(12 + i, tiles[t])
            for k in range(K):
                for f in range(5):
                    band[side, 0, f, k, t, put : put + 16, :] = states[0][f, k, t, first + 8 : first + 24, :]
                    for step in range(1, STEPS):
                        at, start = far[side]
                        band[side, step, f, k, t, at : at + 8, :] = states[step][f, k, t, start + 8 : start + 16, :]
            at = 8 if side == 0 else 24
            rhos = [
                density(band[side, 0, T, k, t, at : at + 8, :], band[side, 0, S, k, t, at : at + 8, :], slope_of(k))
                for k in range(K)
            ]
            for k, value in enumerate(column_pressure(rhos)):
                band[side, 0, PR, k, t, at : at + 8, :] = value
            for at in (8, 16, 24):
                sea = band_geo[side, 1, t, at : at + 8, :] == 1.0
                for k in range(K):
                    wet = sea & (band_geo[side, 0, t, at : at + 8, :] > k)
                    band_wet[side, k, t, at : at + 8, :] = jnp.where(wet, 1.0, 0.0)

    own_rows = slice(OFFSET, top)
    for f in range(4):
        sf[0, f, own_rows, :] = strip_in[f]
    for i in range(5):
        sg[i, own_rows, :] = strip_in[4 + i]
    for side, (at, to) in enumerate(((8, OFFSET - 8), (24, top))):
        for f in range(4):
            sf[0, f, to : to + 8, :] = strip_of(
                [[band[side, 0, f, k, t, at : at + 8, :] for t in range(2)] for k in range(K)]
            )
        for i in range(5):
            sg[i, to : to + 8, :] = strip_of([[band_geo[side, i, t, at : at + 8, :] for t in range(2)]] * K)
    level = lane // 32
    slope = slope_of(level.astype(jnp.float32))

    def strip_pressure(t, s):
        rho = density(t, s, slope)
        one = jnp.where(lane >= 32, pltpu.roll(rho, 32, 1), 0.0)
        two = jnp.where(lane >= 64, pltpu.roll(rho, 64, 1), 0.0)
        return 0.5 * rho + (one + two)

    @pl.loop(0, (rows + 16) // 8, unroll=2)
    def _(b):
        r = pl.multiple_of(OFFSET - 8 + 8 * b, 8)
        at = pl.ds(r, 8)
        west, east = cols[0, at, :], cols[1, at, :]

        def insert(x, planes):
            for k, p in enumerate(planes):
                w = pltpu.roll(west, (32 * k - 4 * p) % LANES, 1)
                e = pltpu.roll(east, (32 * k + 28 - 4 * p) % LANES, 1)
                x = jnp.where((lane >= 32 * k) & (lane < 32 * k + 4), w, x)
                x = jnp.where((lane >= 32 * k + 28) & (lane < 32 * k + 32), e, x)
            return x

        for f in range(4):
            sf[0, f, at, :] = insert(sf[0, f, at, :], (3 * f, 3 * f + 1, 3 * f + 2))
        for i in range(5):
            sg[i, at, :] = insert(sg[i, at, :], (12 + i,) * K)
        sf[0, PR, at, :] = strip_pressure(sf[0, T, at, :], sf[0, S, at, :])
        wet = (sg[1, at, :] == 1.0) & (sg[0, at, :] > level.astype(jnp.float32))
        sw[at, :] = jnp.where(wet, 1.0, 0.0)

    def rolled(c):
        return pltpu.roll(c, LANES - 1, 1), pltpu.roll(c, 1, 1)

    @pl.loop(0, (rows + 16) // 8, unroll=7)
    def _(b):
        r = pl.multiple_of(OFFSET - 8 + 8 * b, 8)
        at = pl.ds(r, 8)
        c = sw[at, :]
        e, w = rolled(c)
        values = coefficients(
            c, e, w, sw[pl.ds(r + 1, 8), :], sw[pl.ds(r - 1, 8), :], sg[2, at, :], sg[3, at, :], sg[4, at, :]
        )
        for i, value in enumerate(values):
            sc[i, at, :] = value

    for side in range(2):
        @pl.loop(0, 2, unroll=2)
        def _(b):
            r = pl.multiple_of(blocks[side][0] + 8 * b, 8)

            def write(i, k, t, value):
                band_coef[side, i, k, t, pl.ds(r, 8), :] = value

            tile_coefficients(
                lambda k, t, row: band_wet[side, k, t, pl.ds(row, 8), :],
                lambda i, t, row: band_geo[side, 2 + i, t, pl.ds(row, 8), :],
                r,
                write,
            )

    for step in range(STEPS):
        final = step == STEPS - 1

        @pl.loop(0, 2 if final else 4, unroll=2 if final else 4)
        def _(n):
            side = n if final else lax.div(n, 2)
            r = pl.multiple_of(16 + 0 * n if final else 8 + 8 * (lax.rem(n, 2) + side), 8)

            def write(f, k, t, value):
                if final:
                    to = pl.multiple_of(side * (rows - 8), 8)
                    outs[f][k, pl.ds(to, 8), tiles[t]] = value
                else:
                    band[side, step + 1, f, k, t, pl.ds(r, 8), :] = value

            advance_tiles(
                lambda f, k, t, row: band[side, step, f, k, t, pl.ds(row, 8), :],
                lambda i, k, t, row: band_coef[side, i, k, t, pl.ds(row, 8), :],
                r,
                write,
                last=final,
            )

    def strip_step(step, r):
        at = pl.ds(r, 8)

        def around(f):
            c = sf[step % 2, f, at, :]
            return (c,) + rolled(c) + (sf[step % 2, f, pl.ds(r + 1, 8), :], sf[step % 2, f, pl.ds(r - 1, 8), :])

        return advance(around, lambda i: sc[i, at, :])

    for step in range(STEPS - 1):
        @pl.loop(0, (rows + 16) // 8, unroll=7)
        def _(b):
            r = pl.multiple_of(OFFSET - 8 + 8 * b, 8)
            new = strip_step(step, r)
            for f in range(4):
                sf[(step + 1) % 2, f, pl.ds(r, 8), :] = new[f]
            sf[(step + 1) % 2, PR, pl.ds(r, 8), :] = strip_pressure(new[T], new[S])

    def finish(q, source):
        new = strip_step(STEPS - 1, q + OFFSET)
        at = pl.ds(q, 8)
        for f in range(4):
            for k in range(K):
                low = pltpu.roll(new[f], (-32 * k - 4) % LANES, 1)
                high = pltpu.roll(new[f], 100 - 32 * k, 1)
                outs[f][k, at, tiles[0]] = jnp.where(lane < HALO, low, source[f][k, at, tiles[0]])
                outs[f][k, at, tiles[1]] = jnp.where(lane >= LANES - HALO, high, source[f][k, at, tiles[1]])

    finish(0, outs)
    finish(rows - 8, outs)

    @pl.loop(1, rows // 8 - 1, unroll=5)
    def _(b):
        finish(pl.multiple_of(8 * b, 8), parts)


def lon_pairs(nlon, nlat, partner):
    return [(i * nlat + j, partner(i) * nlat + j) for i in range(nlon) for j in range(nlat)]


def lat_pairs(nlon, nlat, odd):
    pairs = []
    for i in range(nlon):
        for j in range(nlat):
            up = (j % 2 == 0) != odd
            to, at = (j + 1 if up else j - 1), i
            if to < 0:
                continue
            if to == nlat:
                to, at = nlat - 1, nlon - 1 - i
            pairs.append((i * nlat + j, at * nlat + to))
    return pairs


def body(u_vel, v_vel, temp, salt, levels, land_sea, coriolis, inv_dx, inv_dy):
    args = (u_vel, v_vel, temp, salt, levels, land_sea, coriolis, inv_dx, inv_dy)
    rows, cols = levels.shape
    nlon, nlat = lax.axis_size("lon"), lax.axis_size("lat")
    axes = ("lon", "lat")
    params = pltpu.CompilerParams(vmem_limit_bytes=VMEM_LIMIT)
    f32 = jnp.float32
    column = jax.ShapeDtypeStruct((rows, LANES), f32)
    col_b, col_a = pl.pallas_call(
        pack_columns,
        in_specs=[pl.BlockSpec(memory_space=pltpu.HBM)] * 9,
        out_shape=(column, column),
        scratch_shapes=[pltpu.VMEM(a.shape, a.dtype) for a in args] + [pltpu.SemaphoreType.DMA((9,))],
        compiler_params=pltpu.CompilerParams(vmem_limit_bytes=62 * 1024 * 1024),
        name="pack_columns",
    )(*args)
    col_b = lax.ppermute(
        col_b, axes, lon_pairs(nlon, nlat, lambda i: (i + 1 if i % 2 else i - 1) % nlon)
    )
    col_a = lax.ppermute(col_a, axes, lon_pairs(nlon, nlat, lambda i: i ^ 1))

    state = jax.ShapeDtypeStruct((5, K, 2, rows + 16, LANES), f32)
    vmem = pl.BlockSpec(memory_space=pltpu.VMEM)
    state0, coef, strip = pl.pallas_call(
        prepare_interior,
        in_specs=[vmem] * 9,
        out_shape=(
            state,
            jax.ShapeDtypeStruct((11, K, 2, rows + 16, LANES), f32),
            jax.ShapeDtypeStruct((9, rows, LANES), f32),
        ),
        scratch_shapes=[pltpu.VMEM((K, 2, rows + 16, LANES), f32)],
        compiler_params=params,
        cost_estimate=pl.CostEstimate(flops=10_000_000, bytes_accessed=8_000_000, transcendentals=0),
        name="prepare_interior",
    )(*args)

    def edge(block):
        def spec(a):
            if a.ndim == 3:
                return pl.BlockSpec((K, 8, cols), lambda i: (0, block, 0))
            return pl.BlockSpec((8, cols), lambda i: (block, 0))
        return [spec(a) for a in args]

    whole = pl.BlockSpec((rows, LANES), lambda i: (0, 0))
    row = jax.ShapeDtypeStruct((4 * PLANES + 4, cols), f32)
    row_spec = pl.BlockSpec(row.shape, lambda i: (0, 0))
    row_b, row_a = pl.pallas_call(
        pack_rows,
        grid=(1,),
        in_specs=edge(0) + edge(rows // 8 - 1) + [whole, whole, pl.BlockSpec(memory_space=pl.ANY)],
        out_specs=(row_spec, row_spec),
        out_shape=(row, row),
        compiler_params=params,
        name="pack_rows",
    )(*args, *args, col_b, col_a, strip)
    sent = row_b
    row_b = lax.ppermute(row_b, axes, lat_pairs(nlon, nlat, True))
    row_a = lax.ppermute(row_a, axes, lat_pairs(nlon, nlat, False))
    out = jax.ShapeDtypeStruct(u_vel.shape, f32)
    *kept, = pl.pallas_call(
        run_interior,
        in_specs=[vmem] * 2 + [pl.BlockSpec(memory_space=pl.ANY)],
        out_shape=(state,) * 3 + (out,) * 4,
        compiler_params=params,
        cost_estimate=pl.CostEstimate(flops=30_000_000, bytes_accessed=16_000_000, transcendentals=0),
        name="run_interior",
    )(state0, coef, sent)
    tall = rows + 32
    return pl.pallas_call(
        run_rims,
        out_shape=(out,) * 4,
        scratch_shapes=[
            pltpu.VMEM(row.shape, f32),
            pltpu.VMEM((2, tall, LANES), f32),
            pltpu.VMEM((2, 4, 5, K, 2, 40, LANES), f32),
            pltpu.VMEM((2, 5, 2, 40, LANES), f32),
            pltpu.VMEM((2, K, 2, 40, LANES), f32),
            pltpu.VMEM((2, 11, K, 2, 40, LANES), f32),
            pltpu.VMEM((2, 5, tall, LANES), f32),
            pltpu.VMEM((5, tall, LANES), f32),
            pltpu.VMEM((tall, LANES), f32),
            pltpu.VMEM((11, tall, LANES), f32),
        ],
        compiler_params=params,
        name="run_rims",
    )(*args[4:], state0, *kept, strip, col_b, col_a, row_b, row_a)


def solution(mesh):
    block, plane = P(None, "lat", "lon"), P("lat", "lon")
    return jax.shard_map(
        body,
        mesh=mesh,
        in_specs=(block,) * 4 + (plane,) * 5,
        out_specs=(block,) * 4,
        check_vma=False,
    )
```

```python
import jax
import jax.numpy as jnp
from jax import lax
from jax.experimental import pallas as pl
from jax.experimental.pallas import tpu as pltpu
from jax.sharding import PartitionSpec as P

STEPS = 4
K = 3
HALO = 4
PLANES = 17
LANES = 128
OFFSET = 16
U, V, T, S, PR = range(5)
CXE, CXW, CYN, CYS, HXE, HXW, HYN, HYS, WET, WCEN, WCOR = range(11)
VMEM_LIMIT = 28 * 1024 * 1024


def plane_values(refs, p, rows, lanes):
    if p < 12:
        return refs[p // 3][p % 3, rows, lanes]
    return refs[4 + p - 12][rows, lanes].astype(jnp.float32)


def lane_index(shape):
    return lax.broadcasted_iota(jnp.int32, shape, len(shape) - 1)


def pack_columns(*refs):
    args, (out_b, out_a), ins, sems = refs[:9], refs[9:11], refs[11:20], refs[20]
    copies = [pltpu.make_async_copy(a, i, sems.at[n]) for n, (a, i) in enumerate(zip(args, ins))]
    for copy in copies:
        copy.start()
    rows, cols = ins[4].shape
    even = lax.rem(lax.axis_index("lon"), 2) == 0
    lane = lane_index((8, LANES))
    blocks = range(0, rows, 8)
    west, east = {}, {}
    for p in range(PLANES):
        if p % 3 == 0 or p > 12:
            copies[p // 3 if p < 12 else p - 8].wait()
        for r in blocks:
            w = plane_values(ins, p, slice(r, r + 8), slice(0, LANES))
            e = plane_values(ins, p, slice(r, r + 8), slice(cols - LANES, cols))
            x = pltpu.roll(jnp.where(lane < LANES // 2, w, e), 4 * p + HALO, 1)
            west[r] = jnp.where(lane >= 4 * p + HALO, x, west[r]) if p else x
            east[r] = jnp.where(lane >= 4 * p, x, east[r]) if p else x
    for r in blocks:
        west[r] = pltpu.roll(west[r], LANES - HALO, 1)
    for r in blocks:
        out_a[r : r + 8, :] = jnp.where(even, east[r], west[r])
        out_b[r : r + 8, :] = jnp.where(even, west[r], east[r])


def pack_rows(*refs):
    south, north = refs[0:9], refs[9:18]
    col_b, col_a, _, out_b, out_a = refs[18:]
    rows = col_a.shape[0]
    even = lax.rem(lax.axis_index("lat"), 2) == 0
    for p in range(PLANES):
        s = plane_values(south, p, slice(0, 8), slice(None))[:HALO]
        n = plane_values(north, p, slice(0, 8), slice(None))[HALO:]
        out_a[4 * p : 4 * p + 4, :] = jnp.where(even, n, s)
        out_b[4 * p : 4 * p + 4, :] = jnp.where(even, s, n)
    for ref, lanes in ((col_a, slice(0, LANES)), (col_b, slice(LANES, 2 * LANES))):
        s = ref[0:HALO, :]
        n = ref[rows - HALO : rows, :]
        out_a[4 * PLANES : 4 * PLANES + 4, lanes] = jnp.where(even, n, s)
        out_b[4 * PLANES : 4 * PLANES + 4, lanes] = jnp.where(even, s, n)


def xor_rows(x, bit):
    row = lax.broadcasted_iota(jnp.int32, x.shape, 0)
    return jnp.where((row & bit) != 0, pltpu.roll(x, bit, 0), pltpu.roll(x, 8 - bit, 0))


def xor_lanes(x, bit):
    lane = lane_index(x.shape)
    if bit == LANES // 2:
        return pltpu.roll(x, bit, 1)
    return jnp.where((lane & bit) != 0, pltpu.roll(x, bit, 1), pltpu.roll(x, LANES - bit, 1))


def fold_rows(ref, out):
    lane = lane_index((8, LANES))
    row = lax.broadcasted_iota(jnp.int32, (8, LANES), 0)
    for r in range(0, 4 * PLANES + 4, 8):
        turned, short = [], []
        for t in range(2):
            x = ref[r : r + 8, t * LANES : (t + 1) * LANES]
            x = xor_rows(xor_rows(x, 1), 2)
            x = xor_lanes(xor_lanes(x, 1), 2)
            short.append(x)
            for bit in (4, 8, 16, 32, 64):
                x = xor_lanes(x, bit)
            turned.append(x)
        for t in range(2):
            x = turned[1 - t]
            if r < 24:
                x = -x
            if r + 8 > 4 * PLANES:
                packed = jnp.where(lane < 24, -short[t], short[t])
                x = jnp.where(row < 4, x, packed)
            out[r : r + 8, t * LANES : (t + 1) * LANES] = x


def density(t, s, slope):
    return t * (slope - 0.08 * t - 0.035 * s) + 0.7 * s


def slope_of(level):
    return -0.8 - 0.24 * ((level + 0.5) / K)


def column_pressure(rhos):
    above, out = None, []
    for rho in rhos:
        half = 0.5 * rho
        out.append(half if above is None else above + half)
        above = rho if above is None else above + rho
    return out


def coefficients(c, e, w, n, s, coriolis, idx, idy):
    hx, hy = 0.025 * idx, 0.025 * idy
    hxe, hxw, hyn, hys = c * e * hx, c * w * hx, c * n * hy, c * s * hy
    cx, cy = 1.2 * idx, 1.2 * idy
    cxe, cxw, cyn, cys = hxe * cx, hxw * cx, hyn * cy, hys * cy
    total = (cxe + cxw) + (cyn + cys)
    return cxe, cxw, cyn, cys, hxe, hxw, hyn, hys, c, c - 2.0 * total, 0.1 * c * coriolis


def advance(around, get):
    cxe, cxw, cyn, cys = get(CXE), get(CXW), get(CYN), get(CYS)
    hxe, hxw, hyn, hys = get(HXE), get(HXW), get(HYN), get(HYS)
    us, vs = around(U), around(V)
    u, v = us[0], vs[0]
    u2, v2 = u + u, v + v
    ae, aw = cxe - hxe * u2, cxw + hxw * u2
    an, as_ = cyn - hyn * v2, cys + hys * v2
    ac = get(WET) - ((ae + aw) + (an + as_))
    wcor = get(WCOR)
    p, pe, pw, pn, ps = around(PR)
    px = hxe * (pe - p) + hxw * (p - pw)
    py = hyn * (pn - p) + hys * (p - ps)

    def combine(xs, ac, ae, aw, an, as_):
        c, e, w, n, s = xs
        return (ac * c + (ae * e + aw * w)) + (an * n + as_ * s)

    u_new = combine(us, ac, ae, aw, an, as_) + (wcor * v - px)
    v_new = combine(vs, ac, ae, aw, an, as_) - (wcor * u + py)
    ae = cxe - hxe * (u + us[1])
    aw = cxw + hxw * (u + us[2])
    an = cyn - hyn * (v + vs[3])
    as_ = cys + hys * (v + vs[4])
    ac = get(WCEN) + ((ae + aw) + (an + as_))
    t_new = combine(around(T), ac, ae, aw, an, as_)
    s_new = combine(around(S), ac, ae, aw, an, as_)
    return u_new, v_new, t_new, s_new


def east_west(c, other, t):
    lane = lane_index(c.shape)
    if t == 0:
        e = pltpu.roll(jnp.where(lane == 0, other, c), LANES - 1, 1)
        w = pltpu.roll(c, 1, 1)
    else:
        e = pltpu.roll(c, LANES - 1, 1)
        w = pltpu.roll(jnp.where(lane == LANES - 1, other, c), 1, 1)
    return e, w


def advance_tiles(field, coef, r, write, last=False):
    for t in range(2):
        above = None
        for k in range(K):
            def around(f):
                c = field(f, k, t, r)
                e, w = east_west(c, field(f, k, 1 - t, r), t)
                return c, e, w, field(f, k, t, r + 1), field(f, k, t, r - 1)

            new = advance(around, lambda i: coef(i, k, t, r))
            for f in range(4):
                write(f, k, t, new[f])
            if not last:
                rho = density(new[T], new[S], slope_of(k))
                half = 0.5 * rho
                write(PR, k, t, half if k == 0 else above + half)
                above = rho if k == 0 else above + rho


def tile_coefficients(wet, geo, r, write):
    for k in range(K):
        for t in range(2):
            c = wet(k, t, r)
            e, w = east_west(c, wet(k, 1 - t, r), t)
            values = coefficients(
                c, e, w, wet(k, t, r + 1), wet(k, t, r - 1), geo(0, t, r), geo(1, t, r), geo(2, t, r)
            )
            for i, value in enumerate(values):
                write(i, k, t, value)


def strip_of(tiles):
    lane = lane_index((8, LANES))
    out = None
    for k, (low, high) in enumerate(tiles):
        x = pltpu.roll(low, 32 * k + 4, 1)
        y = pltpu.roll(high, (32 * k - 100) % LANES, 1)
        both = jnp.where(lane >= 32 * k + 16, y, x)
        out = both if k == 0 else jnp.where(lane >= 32 * k, both, out)
    return out


def prepare_interior(*refs):
    ins, (state, coef, strip, after, wet) = refs[:9], refs[9:]
    rows = ins[4].shape[0]
    tiles = [slice(t * LANES, (t + 1) * LANES) for t in range(2)]

    @pl.loop(0, rows // 8, unroll=6)
    def _(b):
        q = pl.multiple_of(8 * b, 8)
        r = pl.multiple_of(8 * b + 8, 8)
        at, own = pl.ds(r, 8), pl.ds(q, 8)
        for f in range(4):
            for k in range(K):
                for t in range(2):
                    state[f, k, t, at, :] = ins[f][k, own, tiles[t]]
            strip[f, own, :] = strip_of([[ins[f][k, own, tiles[t]] for t in range(2)] for k in range(K)])
        for i in range(5):
            strip[4 + i, own, :] = strip_of([[ins[4 + i][own, tiles[t]].astype(jnp.float32) for t in range(2)]] * K)
        for t in range(2):
            sea = ins[5][own, tiles[t]] == 1
            rhos = []
            for k in range(K):
                wet[k, t, at, :] = jnp.where(sea & (ins[4][own, tiles[t]] > k), 1.0, 0.0)
                rhos.append(density(ins[T][k, own, tiles[t]], ins[S][k, own, tiles[t]], slope_of(k)))
            for k, value in enumerate(column_pressure(rhos)):
                state[PR, k, t, at, :] = value

    @pl.loop(0, rows // 8, unroll=6)
    def _(b):
        r = pl.multiple_of(8 * b + 8, 8)

        def write(i, k, t, value):
            coef[i, k, t, pl.ds(r, 8), :] = value

        tile_coefficients(
            lambda k, t, row: wet[k, t, pl.ds(row, 8), :],
            lambda i, t, row: ins[6 + i][pl.ds(pl.multiple_of(8 * b, 8), 8), tiles[t]],
            r,
            write,
        )

    @pl.loop(0, rows // 8, unroll=6)
    def _(b):
        r = pl.multiple_of(8 * b + 8, 8)

        def write(f, k, t, value):
            after[f, k, t, pl.ds(r, 8), :] = value

        advance_tiles(
            lambda f, k, t, row: state[f, k, t, pl.ds(row, 8), :],
            lambda i, k, t, row: coef[i, k, t, pl.ds(row, 8), :],
            r,
            write,
        )


def run_interior(*refs):
    coef, states, outs = refs[1], (None, refs[0]) + refs[3:5], refs[5:9]
    rows = outs[0].shape[1]
    tiles = [slice(t * LANES, (t + 1) * LANES) for t in range(2)]

    for step in range(1, STEPS):
        @pl.loop(0, rows // 8, unroll=6)
        def _(b):
            r = pl.multiple_of(8 * b + 8, 8)

            def write(f, k, t, value):
                if step < STEPS - 1:
                    states[step + 1][f, k, t, pl.ds(r, 8), :] = value
                else:
                    outs[f][k, pl.ds(pl.multiple_of(8 * b, 8), 8), tiles[t]] = value

            advance_tiles(
                lambda f, k, t, row: states[step][f, k, t, pl.ds(row, 8), :],
                lambda i, k, t, row: coef[i, k, t, pl.ds(row, 8), :],
                r,
                write,
                last=step == STEPS - 1,
            )


def run_rims(*refs):
    geo_in, states, parts, strip_in = refs[0:5], refs[5:9], refs[9:13], refs[13]
    col_b, col_a, row_b, row_a = refs[14:18]
    outs = refs[18:22]
    north, cols, band, band_geo, band_wet, band_coef, sf, sg, sw, sc = refs[22:]
    rows = geo_in[0].shape[0]
    top = OFFSET + rows
    lon_even = lax.rem(lax.axis_index("lon"), 2) == 0
    lat = lax.axis_index("lat")
    lat_even = lax.rem(lat, 2) == 0
    lane = lane_index((8, LANES))
    tiles = [slice(t * LANES, (t + 1) * LANES) for t in range(2)]
    fold = lat == lax.axis_size("lat") - 1

    @pl.when(fold)
    def _():
        fold_rows(row_b, north)

    @pl.when(jnp.logical_not(fold))
    def _():
        north[...] = jnp.where(lat_even, row_a[...], row_b[...])

    def south_rows(p, lanes):
        rows_p = slice(4 * p, 4 * p + 4)
        return jnp.where(lat_even, row_b[rows_p, lanes], row_a[rows_p, lanes])

    def north_rows(p, lanes):
        return north[4 * p : 4 * p + 4, lanes]

    def place(dst, a, b):
        cols[0, dst, :] = jnp.where(lon_even, b, a)
        cols[1, dst, :] = jnp.where(lon_even, a, b)

    place(slice(OFFSET, top), col_a[...], col_b[...])
    place(slice(OFFSET - HALO, OFFSET), *(south_rows(PLANES, tiles[i]) for i in range(2)))
    place(slice(top, top + HALO), *(north_rows(PLANES, tiles[i]) for i in range(2)))

    own = ((16, 0), (8, rows - 16))
    far = ((24, 8), (8, rows - 16))
    halo = ((12, south_rows), (24, north_rows))
    blocks = ((8, 16), (16, 24))
    for side in range(2):
        put, first = own[side]
        place_h, rows_of = halo[side]
        for t in range(2):
            for f in range(4):
                for k in range(K):
                    band[side, 0, f, k, t, place_h : place_h + 4, :] = rows_of(3 * f + k, tiles[t])
            for i in range(5):
                band_geo[side, i, t, put : put + 16, :] = geo_in[i][first : first + 16, tiles[t]].astype(jnp.float32)
                band_geo[side, i, t, place_h : place_h + 4, :] = rows_of(12 + i, tiles[t])
            for k in range(K):
                for f in range(5):
                    band[side, 0, f, k, t, put : put + 16, :] = states[0][f, k, t, first + 8 : first + 24, :]
                    for step in range(1, STEPS):
                        at, start = far[side]
                        band[side, step, f, k, t, at : at + 8, :] = states[step][f, k, t, start + 8 : start + 16, :]
            at = 8 if side == 0 else 24
            rhos = [
                density(band[side, 0, T, k, t, at : at + 8, :], band[side, 0, S, k, t, at : at + 8, :], slope_of(k))
                for k in range(K)
            ]
            for k, value in enumerate(column_pressure(rhos)):
                band[side, 0, PR, k, t, at : at + 8, :] = value
            for at in (8, 16, 24):
                sea = band_geo[side, 1, t, at : at + 8, :] == 1.0
                for k in range(K):
                    wet = sea & (band_geo[side, 0, t, at : at + 8, :] > k)
                    band_wet[side, k, t, at : at + 8, :] = jnp.where(wet, 1.0, 0.0)

    own_rows = slice(OFFSET, top)
    for f in range(4):
        sf[0, f, own_rows, :] = strip_in[f]
    for i in range(5):
        sg[i, own_rows, :] = strip_in[4 + i]
    for side, (at, to) in enumerate(((8, OFFSET - 8), (24, top))):
        for f in range(4):
            sf[0, f, to : to + 8, :] = strip_of(
                [[band[side, 0, f, k, t, at : at + 8, :] for t in range(2)] for k in range(K)]
            )
        for i in range(5):
            sg[i, to : to + 8, :] = strip_of([[band_geo[side, i, t, at : at + 8, :] for t in range(2)]] * K)
    level = lane // 32
    slope = slope_of(level.astype(jnp.float32))

    def strip_pressure(t, s):
        rho = density(t, s, slope)
        one = jnp.where(lane >= 32, pltpu.roll(rho, 32, 1), 0.0)
        two = jnp.where(lane >= 64, pltpu.roll(rho, 64, 1), 0.0)
        return 0.5 * rho + (one + two)

    @pl.loop(0, (rows + 16) // 8, unroll=2)
    def _(b):
        r = pl.multiple_of(OFFSET - 8 + 8 * b, 8)
        at = pl.ds(r, 8)
        west, east = cols[0, at, :], cols[1, at, :]

        def insert(x, planes):
            for k, p in enumerate(planes):
                w = pltpu.roll(west, (32 * k - 4 * p) % LANES, 1)
                e = pltpu.roll(east, (32 * k + 28 - 4 * p) % LANES, 1)
                x = jnp.where((lane >= 32 * k) & (lane < 32 * k + 4), w, x)
                x = jnp.where((lane >= 32 * k + 28) & (lane < 32 * k + 32), e, x)
            return x

        for f in range(4):
            sf[0, f, at, :] = insert(sf[0, f, at, :], (3 * f, 3 * f + 1, 3 * f + 2))
        for i in range(5):
            sg[i, at, :] = insert(sg[i, at, :], (12 + i,) * K)
        sf[0, PR, at, :] = strip_pressure(sf[0, T, at, :], sf[0, S, at, :])
        wet = (sg[1, at, :] == 1.0) & (sg[0, at, :] > level.astype(jnp.float32))
        sw[at, :] = jnp.where(wet, 1.0, 0.0)

    def rolled(c):
        return pltpu.roll(c, LANES - 1, 1), pltpu.roll(c, 1, 1)

    @pl.loop(0, (rows + 16) // 8, unroll=7)
    def _(b):
        r = pl.multiple_of(OFFSET - 8 + 8 * b, 8)
        at = pl.ds(r, 8)
        c = sw[at, :]
        e, w = rolled(c)
        values = coefficients(
            c, e, w, sw[pl.ds(r + 1, 8), :], sw[pl.ds(r - 1, 8), :], sg[2, at, :], sg[3, at, :], sg[4, at, :]
        )
        for i, value in enumerate(values):
            sc[i, at, :] = value

    for side in range(2):
        @pl.loop(0, 2, unroll=2)
        def _(b):
            r = pl.multiple_of(blocks[side][0] + 8 * b, 8)

            def write(i, k, t, value):
                band_coef[side, i, k, t, pl.ds(r, 8), :] = value

            tile_coefficients(
                lambda k, t, row: band_wet[side, k, t, pl.ds(row, 8), :],
                lambda i, t, row: band_geo[side, 2 + i, t, pl.ds(row, 8), :],
                r,
                write,
            )

    for step in range(STEPS):
        final = step == STEPS - 1

        @pl.loop(0, 2 if final else 4, unroll=2 if final else 4)
        def _(n):
            side = n if final else lax.div(n, 2)
            r = pl.multiple_of(16 + 0 * n if final else 8 + 8 * (lax.rem(n, 2) + side), 8)

            def write(f, k, t, value):
                if final:
                    to = pl.multiple_of(side * (rows - 8), 8)
                    outs[f][k, pl.ds(to, 8), tiles[t]] = value
                else:
                    band[side, step + 1, f, k, t, pl.ds(r, 8), :] = value

            advance_tiles(
                lambda f, k, t, row: band[side, step, f, k, t, pl.ds(row, 8), :],
                lambda i, k, t, row: band_coef[side, i, k, t, pl.ds(row, 8), :],
                r,
                write,
                last=final,
            )

    def strip_step(step, r):
        at = pl.ds(r, 8)

        def around(f):
            c = sf[step % 2, f, at, :]
            return (c,) + rolled(c) + (sf[step % 2, f, pl.ds(r + 1, 8), :], sf[step % 2, f, pl.ds(r - 1, 8), :])

        return advance(around, lambda i: sc[i, at, :])

    for step in range(STEPS - 1):
        @pl.loop(0, (rows + 16) // 8, unroll=7)
        def _(b):
            r = pl.multiple_of(OFFSET - 8 + 8 * b, 8)
            new = strip_step(step, r)
            for f in range(4):
                sf[(step + 1) % 2, f, pl.ds(r, 8), :] = new[f]
            sf[(step + 1) % 2, PR, pl.ds(r, 8), :] = strip_pressure(new[T], new[S])

    def finish(q, source):
        new = strip_step(STEPS - 1, q + OFFSET)
        at = pl.ds(q, 8)
        for f in range(4):
            for k in range(K):
                low = pltpu.roll(new[f], (-32 * k - 4) % LANES, 1)
                high = pltpu.roll(new[f], 100 - 32 * k, 1)
                outs[f][k, at, tiles[0]] = jnp.where(lane < HALO, low, source[f][k, at, tiles[0]])
                outs[f][k, at, tiles[1]] = jnp.where(lane >= LANES - HALO, high, source[f][k, at, tiles[1]])

    finish(0, outs)
    finish(rows - 8, outs)

    @pl.loop(1, rows // 8 - 1, unroll=5)
    def _(b):
        finish(pl.multiple_of(8 * b, 8), parts)


def lon_pairs(nlon, nlat, partner):
    return [(i * nlat + j, partner(i) * nlat + j) for i in range(nlon) for j in range(nlat)]


def lat_pairs(nlon, nlat, odd):
    pairs = []
    for i in range(nlon):
        for j in range(nlat):
            up = (j % 2 == 0) != odd
            to, at = (j + 1 if up else j - 1), i
            if to < 0:
                continue
            if to == nlat:
                to, at = nlat - 1, nlon - 1 - i
            pairs.append((i * nlat + j, at * nlat + to))
    return pairs


def body(u_vel, v_vel, temp, salt, levels, land_sea, coriolis, inv_dx, inv_dy):
    args = (u_vel, v_vel, temp, salt, levels, land_sea, coriolis, inv_dx, inv_dy)
    rows, cols = levels.shape
    nlon, nlat = lax.axis_size("lon"), lax.axis_size("lat")
    axes = ("lon", "lat")
    params = pltpu.CompilerParams(vmem_limit_bytes=VMEM_LIMIT)
    f32 = jnp.float32
    column = jax.ShapeDtypeStruct((rows, LANES), f32)
    col_b, col_a = pl.pallas_call(
        pack_columns,
        in_specs=[pl.BlockSpec(memory_space=pltpu.HBM)] * 9,
        out_shape=(column, column),
        scratch_shapes=[pltpu.VMEM(a.shape, a.dtype) for a in args] + [pltpu.SemaphoreType.DMA((9,))],
        compiler_params=pltpu.CompilerParams(vmem_limit_bytes=62 * 1024 * 1024),
        name="pack_columns",
    )(*args)
    col_b = lax.ppermute(
        col_b, axes, lon_pairs(nlon, nlat, lambda i: (i + 1 if i % 2 else i - 1) % nlon)
    )
    col_a = lax.ppermute(col_a, axes, lon_pairs(nlon, nlat, lambda i: i ^ 1))

    state = jax.ShapeDtypeStruct((5, K, 2, rows + 16, LANES), f32)
    vmem = pl.BlockSpec(memory_space=pltpu.VMEM)
    state0, coef, strip, state1 = pl.pallas_call(
        prepare_interior,
        in_specs=[vmem] * 9,
        out_shape=(
            state,
            jax.ShapeDtypeStruct((11, K, 2, rows + 16, LANES), f32),
            jax.ShapeDtypeStruct((9, rows, LANES), f32),
            state,
        ),
        scratch_shapes=[pltpu.VMEM((K, 2, rows + 16, LANES), f32)],
        compiler_params=params,
        cost_estimate=pl.CostEstimate(flops=10_000_000, bytes_accessed=8_000_000, transcendentals=0),
        name="prepare_interior",
    )(*args)

    def edge(block):
        def spec(a):
            if a.ndim == 3:
                return pl.BlockSpec((K, 8, cols), lambda i: (0, block, 0))
            return pl.BlockSpec((8, cols), lambda i: (block, 0))
        return [spec(a) for a in args]

    whole = pl.BlockSpec((rows, LANES), lambda i: (0, 0))
    row = jax.ShapeDtypeStruct((4 * PLANES + 4, cols), f32)
    row_spec = pl.BlockSpec(row.shape, lambda i: (0, 0))
    row_b, row_a = pl.pallas_call(
        pack_rows,
        grid=(1,),
        in_specs=edge(0) + edge(rows // 8 - 1) + [whole, whole, pl.BlockSpec(memory_space=pl.ANY)],
        out_specs=(row_spec, row_spec),
        out_shape=(row, row),
        compiler_params=params,
        name="pack_rows",
    )(*args, *args, col_b, col_a, strip)
    sent = row_a
    row_b = lax.ppermute(row_b, axes, lat_pairs(nlon, nlat, True))
    row_a = lax.ppermute(row_a, axes, lat_pairs(nlon, nlat, False))
    out = jax.ShapeDtypeStruct(u_vel.shape, f32)
    *kept, = pl.pallas_call(
        run_interior,
        in_specs=[vmem] * 2 + [pl.BlockSpec(memory_space=pl.ANY)],
        out_shape=(state,) * 2 + (out,) * 4,
        compiler_params=params,
        cost_estimate=pl.CostEstimate(flops=30_000_000, bytes_accessed=16_000_000, transcendentals=0),
        name="run_interior",
    )(state1, coef, sent)
    tall = rows + 32
    return pl.pallas_call(
        run_rims,
        out_shape=(out,) * 4,
        scratch_shapes=[
            pltpu.VMEM(row.shape, f32),
            pltpu.VMEM((2, tall, LANES), f32),
            pltpu.VMEM((2, 4, 5, K, 2, 40, LANES), f32),
            pltpu.VMEM((2, 5, 2, 40, LANES), f32),
            pltpu.VMEM((2, K, 2, 40, LANES), f32),
            pltpu.VMEM((2, 11, K, 2, 40, LANES), f32),
            pltpu.VMEM((2, 5, tall, LANES), f32),
            pltpu.VMEM((5, tall, LANES), f32),
            pltpu.VMEM((tall, LANES), f32),
            pltpu.VMEM((11, tall, LANES), f32),
        ],
        compiler_params=params,
        name="run_rims",
    )(*args[4:], state0, state1, *kept, strip, col_b, col_a, row_b, row_a)


def solution(mesh):
    block, plane = P(None, "lat", "lon"), P("lat", "lon")
    return jax.shard_map(
        body,
        mesh=mesh,
        in_specs=(block,) * 4 + (plane,) * 5,
        out_specs=(block,) * 4,
        check_vma=False,
    )
```
